256 devices in a mesh: grp: 8 (over z), dom: 32 (over y, x, core).
Axes of the slice: x: 4, y: 4, z: 8, core: 2. Of those that a mesh axis runs over, the one named last changes fastest.
Arguments:
- local_inverse: bfloat16 [1280, 640, 640], P(('grp', 'dom')), may hold values from -0.25 to 0.25
- local_trace: bfloat16 [1280, 640, 480], P(('grp', 'dom')), may hold values from -0.25 to 0.25
- trace_local: bfloat16 [1280, 480, 640], P(('grp', 'dom')), may hold values from -0.25 to 0.25
- trace_trace: bfloat16 [1280, 480, 480], P(('grp', 'dom')), may hold values from -0.25 to 0.25
- local_rhs: bfloat16 [1280, 640], P(('grp', 'dom')), may hold values from -6 to 6
- trace_rhs: bfloat16 [1280, 480], P(('grp', 'dom')), may hold values from -6 to 6
- trace_state: bfloat16 [3840, 80], P(('grp', 'dom')), may hold values from -6 to 6
- side_owner: int32 [1280, 6], P(('grp', 'dom')), may hold values from 0 to 255, as said below
- side_slot: int32 [1280, 6], P(('grp', 'dom')), may hold values from 0 to 1, as said below
- face_slots: int32 [3840, 2], P(('grp', 'dom')), may hold values from 0 to 63, as said below
Outputs:
- residual: float32 [3840, 80], P(('grp', 'dom'))
- image: float32 [3840, 80], P(('grp', 'dom'))
The draws below stay inside these ranges and needn't reach their ends.
Inputs may be any that keep to these rules, and one draw needn't show every extreme that they name: `side_owner`: an element on the device with grp index g and dom index d has every side owned by a device of grp index g or (g + 1) mod 8; exactly 15 of one device's sides have their owner in each of the two rows. `side_slot`: Take, at grp index g and dom index d, the sides of that device's elements owned in row g together with the sides of the device at grp index (g - 1) mod 8 and the same dom index owned in row g: among those with their owner at one dom index, the slots are distinct. Every element side's receive position is named by exactly one entry of face_slots at its owner, and every entry names one side; each face has two sides of different elements.
All inputs are finite; a program needn't handle non-finite values.
Results may differ from the reference program's by a relative error of at most 0.0065.
Values may be sent and summed in bfloat16 or wider, within the bound.
No kernel may reach another device: no remote copies, remote signals or barrier semaphores. Data moves between devices by JAX's collectives and lax.ppermute only.
A program may use at most 64 MiB of HBM per device.

```python
import jax
import jax.numpy as jnp
from jax import lax

NL = 640
FD = 80
NT = 480
E_DEV = 5
F_DEV = 15
CAP = 2
ELEMS = 1280
FACES = 3840
N_GRP = 8
N_DOM = 32
DEVICES = 256


def build_routes(key):
    half = CAP // 2
    first, second, third = jax.random.split(jax.random.fold_in(key, 7), 3)
    ranking = jax.random.permutation(first, N_DOM).astype(jnp.int32)
    dom_values = jnp.arange(N_DOM, dtype=jnp.int32)
    scores = jnp.where(dom_values == 1, -3, jnp.where(dom_values == N_DOM - 1, -2, jnp.where(dom_values == N_DOM // 2, -1, ranking))).astype(jnp.int32)
    dom_order = jnp.argsort(scores, stable=True).astype(jnp.int32)
    index_face = jnp.arange(F_DEV, dtype=jnp.int32)
    offsets = dom_order[index_face % N_DOM]
    repeat_rank = index_face // N_DOM
    face_order = jax.random.permutation(second, F_DEV).astype(jnp.int32)
    devices_ids = jnp.arange(DEVICES, dtype=jnp.int32)
    grp_ids = devices_ids // N_DOM
    dom_ids = devices_ids % N_DOM
    side_order = jax.vmap(lambda sub: jax.random.permutation(sub, 2 * F_DEV))(jax.random.split(third, DEVICES)).astype(jnp.int32)
    kinds = jnp.arange(2 * F_DEV, dtype=jnp.int32)
    kind_face = kinds % F_DEV
    upper = (kinds >= F_DEV).astype(jnp.int32)
    owner_grp = (grp_ids[:, None] + upper[None, :]) % N_GRP
    owner_dom = (dom_ids[:, None] + offsets[kind_face][None, :]) % N_DOM
    owner = owner_grp * N_DOM + owner_dom
    slot = jnp.broadcast_to(repeat_rank[kind_face] + half * upper, (DEVICES, 2 * F_DEV))
    rows = jnp.broadcast_to(devices_ids[:, None], (DEVICES, 2 * F_DEV))
    owner_sides = jnp.zeros((DEVICES, 2 * F_DEV), jnp.int32).at[rows, side_order].set(owner)
    slot_sides = jnp.zeros((DEVICES, 2 * F_DEV), jnp.int32).at[rows, side_order].set(slot)
    next_face = (index_face + 1) % F_DEV
    lower_pos = (dom_ids[:, None] - offsets[None, :]) % N_DOM * CAP + repeat_rank[None, :]
    upper_pos = (dom_ids[:, None] - offsets[next_face][None, :]) % N_DOM * CAP + half + repeat_rank[next_face][None, :]
    pairs = jnp.stack([lower_pos, upper_pos], axis=2)
    face_table = jnp.zeros((DEVICES, F_DEV, 2), jnp.int32).at[:, face_order, :].set(pairs)
    return (owner_sides.reshape(DEVICES * E_DEV, 6), slot_sides.reshape(DEVICES * E_DEV, 6), face_table.reshape(DEVICES * F_DEV, 2))


def draw_side_owner(key, part):
    return build_routes(key)[0]


def draw_side_slot(key, part):
    return build_routes(key)[1]


def draw_face_slots(key, part):
    return build_routes(key)[2]


def shard_levels(rng, extent, cuts, low, high):
    level = 1.0
    for position, blocks in cuts:
        draws = jax.random.uniform(jax.random.fold_in(jax.random.fold_in(rng, 6), position), (blocks,), jnp.float32, low / len(cuts), high / len(cuts))
        level = level * jnp.repeat(jnp.exp(draws), extent[position] // blocks).reshape((-1,) + (1,) * (len(extent) - 1 - position))
    return level


def centred(own_key, shape, spread, bound, cuts=(), kind=jnp.bfloat16):
    entries = spread * jax.random.normal(own_key, shape, jnp.float32)
    if cuts:
        entries = entries * shard_levels(own_key, shape, cuts, -0.22, 0.18)
    return jnp.clip(entries, -bound, bound).astype(kind)


def setup_inputs(seed: int = 0) -> dict:
    keys = jax.random.split(jax.random.key(seed), 11)
    local_inverse = centred(keys[0], (ELEMS, NL, NL), NL ** -0.5, 0.25, ((0, 256),))
    local_trace = centred(keys[1], (ELEMS, NL, NT), NT ** -0.5, 0.25, ((0, 256),))
    trace_local = centred(keys[2], (ELEMS, NT, NL), NL ** -0.5, 0.25, ((0, 256),))
    trace_trace = centred(keys[3], (ELEMS, NT, NT), NT ** -0.5, 0.25, ((0, 256),))
    local_rhs = centred(keys[4], (ELEMS, NL), 1.0, 6.0, ((0, 256),))
    trace_rhs = centred(keys[5], (ELEMS, NT), 1.0, 6.0, ((0, 256),))
    trace_state = centred(keys[6], (FACES, FD), 1.0, 6.0, ((0, 256),))
    side_owner = draw_side_owner(jax.random.fold_in(keys[10], 71), 0)
    side_slot = draw_side_slot(jax.random.fold_in(keys[10], 71), 0)
    face_slots = draw_face_slots(jax.random.fold_in(keys[10], 71), 0)
    return {"local_inverse": local_inverse, "local_trace": local_trace, "trace_local": trace_local, "trace_trace": trace_trace, "local_rhs": local_rhs, "trace_rhs": trace_rhs, "trace_state": trace_state, "side_owner": side_owner, "side_slot": side_slot, "face_slots": face_slots}


def condense(block):
    inverse, coupling, back, diagonal, interior, boundary = block
    coupled = jnp.einsum('eij,ejk->eik', inverse.astype(jnp.float32), coupling.astype(jnp.float32)).astype(jnp.bfloat16)
    coupled = lax.optimization_barrier(coupled)
    solved = jnp.einsum('eij,ej->ei', inverse.astype(jnp.float32), interior.astype(jnp.float32)).astype(jnp.bfloat16)
    solved = lax.optimization_barrier(solved)
    schur = diagonal.astype(jnp.float32) - jnp.einsum('eij,ejk->eik', back.astype(jnp.float32), coupled.astype(jnp.float32))
    condensed = boundary.astype(jnp.float32) - jnp.einsum('eij,ej->ei', back.astype(jnp.float32), solved.astype(jnp.float32))
    return schur.astype(jnp.bfloat16), condensed.astype(jnp.bfloat16)


def reference(local_inverse, local_trace, trace_local, trace_trace, local_rhs, trace_rhs, trace_state, side_owner, side_slot, face_slots):
    positions = N_DOM * CAP
    elements = E_DEV * DEVICES
    arrays = (local_inverse, local_trace, trace_local, trace_trace, local_rhs, trace_rhs)
    blocks = tuple(item.reshape((DEVICES, E_DEV) + item.shape[1:]) for item in arrays)
    schur, condensed = lax.map(condense, blocks)
    condensed = condensed.reshape(elements, NT)
    element_ids = jnp.arange(elements).astype(jnp.int32)
    holder_dom = (element_ids // E_DEV) % N_DOM
    receive = (side_owner * positions + holder_dom[:, None] * CAP + side_slot).reshape(-1).astype(jnp.int32)
    face_owner = (jnp.arange(FACES).astype(jnp.int32) // F_DEV).astype(jnp.int32)
    face_pos = (face_owner[:, None] * positions + face_slots).astype(jnp.int32)
    face_ids = jnp.repeat(jnp.arange(FACES).astype(jnp.int32), 2)
    pos_face = jnp.zeros((DEVICES * positions,), jnp.int32).at[face_pos.reshape(-1)].set(face_ids)
    side_face = pos_face[receive]

    def apply(vector):
        gathered = vector[side_face].reshape(DEVICES, E_DEV, NT)

        def one(pair):
            blocks_dev, values = pair
            return jnp.einsum('ekj,ej->ek', blocks_dev.astype(jnp.float32), values.astype(jnp.float32))

        return lax.map(one, (schur, gathered)).reshape(elements, NT)

    def assemble(terms):
        arrived = jnp.zeros((DEVICES * positions, FD), jnp.float32).at[receive].add(terms.reshape(-1, FD))
        return arrived[face_pos[:, 0]] + arrived[face_pos[:, 1]]

    residual = assemble(apply(trace_state) - condensed.astype(jnp.float32))
    direction = residual.astype(jnp.bfloat16)
    image = assemble(apply(direction))
    return residual, image
```

```python
import jax
import jax.numpy as jnp
from jax import lax
from jax.experimental import pallas as pl
from jax.experimental.pallas import tpu as pltpu
from jax.sharding import PartitionSpec as P

BF = jnp.bfloat16
F32 = jnp.float32
LANES = 128
SIDES = 6
GROUP = 8
ROWS = SIDES * GROUP
BLOCK = 16
EXACT = lax.Precision.HIGHEST
FACE_LANE = 80


def iota(shape, dim):
    return lax.broadcasted_iota(jnp.int32, shape, dim)


def params(mib=12):
    return pltpu.CompilerParams(vmem_limit_bytes=mib * 1024 * 1024)


def shift(payload, by):
    devices = lax.axis_size("grp")
    return lax.ppermute(payload, "grp", [(i, (i + by) % devices) for i in range(devices)])


def exchange(payload):
    return lax.all_to_all(payload, "dom", split_axis=0, concat_axis=0, tiled=True)


def face_onehot(slots_ref, scratch, positions):
    scratch[...] = jnp.full(scratch.shape, -1, jnp.int32)
    scratch[:, : slots_ref.shape[1]] = slots_ref[...]
    place = iota((positions, BLOCK), 0)
    hit = (place == scratch[0:1, :]) | (place == scratch[1:2, :])
    return jnp.where(hit, 1.0, 0.0)


def spread_kernel(slots_ref, state_ref, out_ref, slots, rows):
    faces, width = state_ref.shape
    rows[...] = jnp.zeros(rows.shape, F32)
    rows[:faces, :width] = state_ref[...].astype(F32)
    lane = iota(rows.shape, 1)
    index = iota(rows.shape, 0).astype(F32)
    table = jnp.where(lane == FACE_LANE, index, rows[...]).astype(BF)
    onehot = face_onehot(slots_ref, slots, out_ref.shape[0]).astype(BF)
    out_ref[...] = jnp.dot(onehot, table, preferred_element_type=F32).astype(BF)


def spread(slots, state, positions):
    return pl.pallas_call(
        spread_kernel,
        out_shape=jax.ShapeDtypeStruct((positions, LANES), BF),
        scratch_shapes=[pltpu.VMEM((2, BLOCK), jnp.int32), pltpu.VMEM((BLOCK, LANES), F32)],
        compiler_params=params(4),
        name="spread",
    )(slots, state)


def routes_kernel(
    grp_count, dom_count, owner_ref, slot_ref, pick_ref, put_ref, compact_ref, own_ref, up_ref, down_ref, key_ref, owners, slots
):
    elements = owner_ref.shape[0]
    owners[...] = jnp.full(owners.shape, -1, jnp.int32)
    slots[...] = jnp.zeros(slots.shape, jnp.int32)
    owners[:elements, :SIDES] = owner_ref[...]
    slots[:elements, :SIDES] = slot_ref[...]

    def rows(ref):
        return jnp.concatenate([jnp.broadcast_to(ref[:, k : k + 1], (GROUP, LANES)) for k in range(SIDES)], axis=0)

    owner = rows(owners)
    slot = rows(slots)
    grp = lax.axis_index("grp")
    parity = lax.axis_index("dom") % 2
    valid = owner >= 0
    owner = jnp.maximum(owner, 0)
    owner_dom = lax.rem(owner, dom_count)
    owner_grp = lax.div(owner, dom_count)
    lifted = valid & (owner_grp != grp)
    held = valid & (owner_grp == grp)
    lane = iota((ROWS, LANES), 1)
    code = owner_dom * 2 + slot + jnp.where(lifted, 2 * dom_count, 0)
    pick = jnp.where(valid & (lane == code), 1.0, 0.0)
    pick_ref[...] = pick.astype(BF)
    pad = jnp.zeros((LANES - ROWS, LANES), F32)
    put_ref[...] = jnp.concatenate([pick, pad], axis=0).T[:, :ROWS]
    before = jnp.where(iota((ROWS, ROWS), 1) < iota((ROWS, ROWS), 0), 1.0, 0.0).astype(BF)

    def rank(flag):
        counts = jnp.dot(before, jnp.where(flag, 1.0, 0.0).astype(BF), preferred_element_type=F32)
        return counts.astype(jnp.int32)

    order = jnp.where(lifted, rank(lifted), rank(held))
    seat = valid & (lane == order + jnp.where(lifted, BLOCK, 0))
    compact = jnp.concatenate([jnp.where(seat, 1.0, 0.0), pad], axis=0).T
    compact_ref[...] = compact[: 2 * BLOCK, :ROWS].astype(BF)
    power = jnp.full((ROWS, LANES), 2.0**-16, F32)
    for bit in range(5):
        power = power * jnp.where((owner_dom & (1 << bit)) != 0, 2.0 ** (1 << bit), 1.0)
    signed = jnp.where(lifted, -power, power)
    base = parity * (4 * BLOCK)
    own_ref[...] = jnp.where(valid & (lane == order + base + jnp.where(lifted, BLOCK, 0)), signed, 0.0)
    up_ref[...] = jnp.where(lifted & (lane == order + base + 2 * BLOCK), power, 0.0)
    down_ref[...] = jnp.where(held & (lane == order + base + 3 * BLOCK), -power, 0.0)
    key_ref[...] = jnp.where(valid, signed, 2.0**-40)


def routes(grp_count, dom_count, owner, slot):
    def table(rows, columns, dtype):
        return jax.ShapeDtypeStruct((rows, columns), dtype)

    full = table(ROWS, LANES, F32)

    def kernel(*refs):
        routes_kernel(grp_count, dom_count, *refs)

    return pl.pallas_call(
        kernel,
        out_shape=(
            table(ROWS, LANES, BF),
            table(LANES, ROWS, F32),
            table(2 * BLOCK, ROWS, BF),
            full,
            full,
            full,
            full,
        ),
        scratch_shapes=[pltpu.VMEM((GROUP, LANES), jnp.int32), pltpu.VMEM((GROUP, LANES), jnp.int32)],
        compiler_params=params(4),
        name="routes",
    )(owner, slot)


def transposed(left, right):
    return lax.dot_general(left, right, (((1,), (1,)), ((), ())), preferred_element_type=F32)


def condense_kernel(inverse_ref, couple_ref, back_ref, diagonal_ref, interior_ref, boundary_ref, schur_ref, condensed_ref):
    e = pl.program_id(0)
    width = diagonal_ref.shape[1]

    def row(ref):
        values = ref[...].astype(F32)
        return jnp.sum(jnp.where(iota(values.shape, 0) == e, values, 0.0), axis=0, keepdims=True)

    right = row(interior_ref)
    right = jnp.broadcast_to(right, (BLOCK, right.shape[1])).astype(BF)
    stacked = jnp.concatenate([couple_ref[0], right], axis=0)
    coupled = transposed(stacked, inverse_ref[0]).astype(BF)
    product = transposed(coupled, back_ref[0])
    schur_ref[0] = (diagonal_ref[0].astype(F32).T - product[:width]).astype(BF)
    condensed = (row(boundary_ref) - product[width : width + 1]).astype(BF).astype(F32)

    @pl.when(e == 0)
    def _():
        condensed_ref[...] = jnp.zeros(condensed_ref.shape, F32)

    here = iota(condensed_ref.shape, 0) == e
    condensed_ref[...] = jnp.where(here, condensed, condensed_ref[...])


def condense(inverse, couple, back, diagonal, interior, boundary):
    elements, inner, _ = inverse.shape
    width = diagonal.shape[1]

    def block(rows, columns):
        return pl.BlockSpec((1, rows, columns), lambda e: (e, 0, 0))

    def whole(array):
        return pl.BlockSpec(array.shape, lambda e: (0, 0))

    flops = 2 * elements * (inner * inner * width + inner * width * width)
    return pl.pallas_call(
        condense_kernel,
        grid=(elements,),
        in_specs=[
            block(inner, inner),
            block(width, inner),
            block(width, inner),
            block(width, width),
            whole(interior),
            whole(boundary),
        ],
        out_specs=(block(width, width), pl.BlockSpec((GROUP, width), lambda e: (0, 0))),
        out_shape=(
            jax.ShapeDtypeStruct((elements, width, width), BF),
            jax.ShapeDtypeStruct((GROUP, width), F32),
        ),
        compiler_params=params(24),
        cost_estimate=pl.CostEstimate(flops=flops, bytes_accessed=15_000_000, transcendentals=0),
        name="condense",
    )(inverse, couple, back, diagonal, interior, boundary)


def products(vectors, schur_ref):
    terms = jnp.zeros(vectors.shape, F32)
    for e in range(schur_ref.shape[0]):
        part = jnp.dot(vectors, schur_ref[e], preferred_element_type=F32)
        terms = jnp.where(iota(terms.shape, 0) == e, part, terms)
    return terms


def gather_wide(values, wide, face_width):
    for k in range(SIDES):
        wide[:, k * face_width : (k + 1) * face_width] = values[k * GROUP : (k + 1) * GROUP, :face_width]
    return wide[...].astype(BF)


def split_rows(terms, wide, tall, face_width):
    wide[...] = terms
    tall[...] = jnp.zeros(tall.shape, F32)
    for k in range(SIDES):
        tall[k * GROUP : (k + 1) * GROUP, :face_width] = wide[:, k * face_width : (k + 1) * face_width]
    return tall[...]


def first_kernel(
    face_width,
    here_ref,
    above_ref,
    schur_ref,
    condensed_ref,
    pick_ref,
    compact_ref,
    own_ref,
    up_ref,
    down_ref,
    key_ref,
    own_out,
    up_out,
    down_out,
    terms_out,
    key_out,
    wide,
    tall,
):
    table = jnp.concatenate([here_ref[...], above_ref[...]], axis=0)
    values = jnp.dot(pick_ref[...], table, preferred_element_type=F32)
    face = 16.0 + jnp.broadcast_to(values[:, FACE_LANE : FACE_LANE + 1], values.shape)
    vectors = gather_wide(values, wide, face_width)
    terms = products(vectors, schur_ref) - condensed_ref[...]
    rows = split_rows(terms, wide, tall, face_width)
    terms_out[...] = rows
    key_out[...] = face * key_ref[...]
    packed = jnp.dot(compact_ref[...], rows.astype(BF), preferred_element_type=F32)

    def key_row(ref):
        return jnp.sum(face * ref[...], axis=0, keepdims=True)

    last = iota((BLOCK, LANES), 0) == BLOCK - 1
    lane = iota((1, LANES), 1)
    own = key_row(own_ref)
    in_first = lax.rem(lane, 4 * BLOCK) < BLOCK
    held = packed[:BLOCK]
    lifted = packed[BLOCK:]
    own_out[:BLOCK] = jnp.where(last, jnp.where(in_first, own, 0.0), held).astype(BF)
    own_out[BLOCK:] = jnp.where(last, jnp.where(in_first, 0.0, own), lifted).astype(BF)
    up_out[...] = jnp.where(last, key_row(up_ref), lifted).astype(BF)
    down_out[...] = jnp.where(last, key_row(down_ref), held).astype(BF)


def first_terms(face_width, *arrays):
    width = arrays[2].shape[1]

    def kernel(*refs):
        first_kernel(face_width, *refs)

    return pl.pallas_call(
        kernel,
        out_shape=(
            jax.ShapeDtypeStruct((2 * BLOCK, LANES), BF),
            jax.ShapeDtypeStruct((BLOCK, LANES), BF),
            jax.ShapeDtypeStruct((BLOCK, LANES), BF),
            jax.ShapeDtypeStruct((ROWS, LANES), F32),
            jax.ShapeDtypeStruct((ROWS, LANES), F32),
        ),
        scratch_shapes=[pltpu.VMEM((GROUP, width), F32), pltpu.VMEM((ROWS, LANES), F32)],
        compiler_params=params(),
        name="first_terms",
    )(*arrays)


def second_kernel(face_width, slab_ref, terms_ref, key_ref, schur_ref, put_ref, held_out, lifted_out, wide, tall):
    depth = slab_ref.shape[0]
    pairs = depth // LANES
    slab = slab_ref[...]
    column = iota((BLOCK, depth), 1)
    chosen = (lax.div(column, LANES) == iota((BLOCK, depth), 0)) & (lax.rem(column, BLOCK) == BLOCK - 1)
    keys = jnp.dot(jnp.where(chosen, 1.0, 0.0).astype(BF), slab, preferred_element_type=F32)
    key = key_ref[...]
    match = jnp.concatenate([jnp.where(key == keys[i : i + 1], 1.0, 0.0).astype(BF) for i in range(pairs)], axis=1)
    first = terms_ref[...]
    both = jnp.dot(match, slab, preferred_element_type=F32)
    residual = both + (first - first.astype(BF).astype(F32))
    vectors = gather_wide(residual.astype(BF).astype(F32), wide, face_width)
    second = split_rows(products(vectors, schur_ref), wide, tall, face_width)
    pair = jnp.concatenate([first, second], axis=1)
    placed = jnp.dot(put_ref[...], pair, preferred_element_type=F32, precision=EXACT)
    positions = held_out.shape[0]
    held_out[...] = placed[:positions]
    lifted_out[...] = placed[positions:]


def second_terms(face_width, positions, *arrays):
    width = arrays[3].shape[1]

    def kernel(*refs):
        second_kernel(face_width, *refs)

    placed = jax.ShapeDtypeStruct((positions, 2 * LANES), F32)
    return pl.pallas_call(
        kernel,
        out_shape=(placed, placed),
        scratch_shapes=[pltpu.VMEM((GROUP, width), F32), pltpu.VMEM((ROWS, LANES), F32)],
        compiler_params=params(),
        name="second_terms",
    )(*arrays)


def collect_kernel(arrived_ref, slots_ref, residual_ref, image_ref, slots):
    faces, width = residual_ref.shape
    onehot = face_onehot(slots_ref, slots, arrived_ref.shape[0])
    total = lax.dot_general(
        onehot, arrived_ref[...], (((0,), (0,)), ((), ())), preferred_element_type=F32, precision=EXACT
    )
    residual_ref[...] = total[:faces, :width]
    image_ref[...] = total[:faces, LANES : LANES + width]


def collect(arrived, slots, faces, width):
    out = jax.ShapeDtypeStruct((faces, width), F32)
    return pl.pallas_call(
        collect_kernel,
        out_shape=(out, out),
        scratch_shapes=[pltpu.VMEM((2, BLOCK), jnp.int32)],
        compiler_params=params(4),
        name="collect",
    )(arrived, slots)


def on_device(
    local_inverse,
    local_trace,
    trace_local,
    trace_trace,
    local_rhs,
    trace_rhs,
    trace_state,
    side_owner,
    side_slot,
    face_slots,
):
    grp_count = lax.axis_size("grp")
    dom_count = lax.axis_size("dom")
    faces, face_width = trace_state.shape
    positions = 2 * dom_count
    slots = face_slots.T
    outgoing = spread(slots, trace_state, positions)
    outgoing, side_owner, side_slot = lax.optimization_barrier((outgoing, side_owner, side_slot))
    here = exchange(outgoing.reshape(dom_count, 2, LANES)).reshape(positions, LANES)
    pick, put, compact, own_keys, up_keys, down_keys, keys = routes(grp_count, dom_count, side_owner, side_slot)
    schur, condensed = condense(
        local_inverse, jnp.swapaxes(local_trace, 1, 2), trace_local, trace_trace, local_rhs, trace_rhs
    )
    above = shift(here, -1)
    own, lifted, held, terms, key = first_terms(
        face_width, here, above, schur, condensed, pick, compact, own_keys, up_keys, down_keys, keys
    )
    rows = jnp.concatenate([own, shift(lifted, 1), shift(held, -1)], axis=0)
    rows = jnp.broadcast_to(rows[None], (dom_count,) + rows.shape)
    slab = exchange(rows).reshape(-1, LANES)
    stay, rise = second_terms(face_width, positions, slab, terms, key, schur, put)
    arriving = stay + shift(rise, 1)
    arrived = exchange(arriving.reshape(dom_count, 2, 2 * LANES)).reshape(positions, 2 * LANES)
    return collect(arrived, slots, faces, face_width)


def solution(mesh):
    both = ("grp", "dom")
    blocks = (P(both, None, None),) * 4
    rows = (P(both, None),) * 6
    return jax.shard_map(
        on_device,
        mesh=mesh,
        in_specs=blocks + rows,
        out_specs=(P(both, None), P(both, None)),
        check_vma=False,
    )
```

```python
import jax
import jax.numpy as jnp
from jax import lax
from jax.experimental import pallas as pl
from jax.experimental.pallas import tpu as pltpu
from jax.sharding import PartitionSpec as P

BF = jnp.bfloat16
F32 = jnp.float32
LANES = 128
SIDES = 6
GROUP = 8
ROWS = SIDES * GROUP
BLOCK = 16
EXACT = lax.Precision.HIGHEST
FACE_LANE = 80
KEY_LANE = 64


def iota(shape, dim):
    return lax.broadcasted_iota(jnp.int32, shape, dim)


def params(mib=12):
    return pltpu.CompilerParams(vmem_limit_bytes=mib * 1024 * 1024)


def in_hbm(*arrays):
    return [pltpu.with_memory_space_constraint(array, pltpu.HBM) for array in arrays]


def shift(payload, by):
    devices = lax.axis_size("grp")
    return lax.ppermute(payload, "grp", [(i, (i + by) % devices) for i in range(devices)])


def exchange(payload):
    return lax.all_to_all(payload, "dom", split_axis=0, concat_axis=0, tiled=True)


def face_onehot(slots_ref, scratch, positions):
    scratch[...] = jnp.full(scratch.shape, -1, jnp.int32)
    scratch[:, : slots_ref.shape[1]] = slots_ref[...]
    place = iota((positions, BLOCK), 0)
    hit = (place == scratch[0:1, :]) | (place == scratch[1:2, :])
    return jnp.where(hit, 1.0, 0.0)


def spread_kernel(slots_from, state_from, out_ref, slots_ref, state_ref, slots, rows, sems):
    copies = [
        pltpu.make_async_copy(slots_from, slots_ref, sems.at[0]),
        pltpu.make_async_copy(state_from, state_ref, sems.at[1]),
    ]
    for copy in copies:
        copy.start()
    for copy in copies:
        copy.wait()
    faces, width = state_ref.shape
    rows[...] = jnp.zeros(rows.shape, F32)
    rows[:faces, :width] = state_ref[...].astype(F32)
    lane = iota(rows.shape, 1)
    index = iota(rows.shape, 0).astype(F32)
    table = jnp.where(lane == FACE_LANE, index, rows[...]).astype(BF)
    onehot = face_onehot(slots_ref, slots, out_ref.shape[0]).astype(BF)
    out_ref[...] = jnp.dot(onehot, table, preferred_element_type=F32).astype(BF)


def spread(slots, state, positions):
    return pl.pallas_call(
        spread_kernel,
        in_specs=[pl.BlockSpec(memory_space=pltpu.HBM)] * 2,
        out_shape=jax.ShapeDtypeStruct((positions, LANES), BF),
        scratch_shapes=[
            pltpu.VMEM(slots.shape, slots.dtype),
            pltpu.VMEM(state.shape, state.dtype),
            pltpu.VMEM((2, BLOCK), jnp.int32),
            pltpu.VMEM((BLOCK, LANES), F32),
            pltpu.SemaphoreType.DMA((2,)),
        ],
        compiler_params=params(4),
        name="spread",
    )(*in_hbm(slots, state))


def fill_routes(
    dom_count, owner_ref, slot_ref, pick_ref, put_ref, compact_ref, code_ref, own_ref, up_ref, down_ref, key_ref, owners, slots
):
    elements = owner_ref.shape[0]
    owners[...] = jnp.full(owners.shape, -1, jnp.int32)
    slots[...] = jnp.zeros(slots.shape, jnp.int32)
    owners[:elements, :SIDES] = owner_ref[...]
    slots[:elements, :SIDES] = slot_ref[...]

    def rows(ref):
        return jnp.concatenate([jnp.broadcast_to(ref[:, k : k + 1], (GROUP, LANES)) for k in range(SIDES)], axis=0)

    owner = rows(owners)
    slot = rows(slots)
    grp = lax.axis_index("grp")
    part = lax.axis_index("dom") % 4
    valid = owner >= 0
    owner = jnp.maximum(owner, 0)
    owner_dom = lax.rem(owner, dom_count)
    owner_grp = lax.div(owner, dom_count)
    lifted = valid & (owner_grp != grp)
    held = valid & (owner_grp == grp)
    lane = iota((ROWS, LANES), 1)
    place = owner_dom * 2 + slot
    pick = jnp.where(valid & (lane == place + jnp.where(lifted, 2 * dom_count, 0)), 1.0, 0.0)
    pick_ref[...] = pick.astype(BF)
    pad = jnp.zeros((LANES - ROWS, LANES), F32)
    put_ref[: 2 * dom_count] = jnp.concatenate([pick, pad], axis=0).T[: 2 * dom_count, :ROWS].astype(BF)
    before = jnp.where(iota((ROWS, ROWS), 1) < iota((ROWS, ROWS), 0), 1.0, 0.0).astype(BF)

    def rank(flag):
        counts = jnp.dot(before, jnp.where(flag, 1.0, 0.0).astype(BF), preferred_element_type=F32)
        return counts.astype(jnp.int32)

    order = jnp.where(lifted, rank(lifted), rank(held))
    seat = valid & (lane == order + jnp.where(lifted, BLOCK, 0))
    compact = jnp.concatenate([jnp.where(seat, 1.0, 0.0), pad], axis=0).T
    compact_ref[...] = compact[: 2 * BLOCK, :ROWS].astype(BF)
    put_ref[2 * dom_count :] = compact[BLOCK : 2 * BLOCK, :ROWS].astype(BF)
    code = jnp.where(lifted & (lane == order), place.astype(F32) + 1.0, 0.0)
    code_ref[...] = jnp.broadcast_to(jnp.sum(code, axis=0, keepdims=True) - 1.0, code_ref.shape)
    power = jnp.full((ROWS, LANES), 2.0**-16, F32)
    for bit in range(5):
        power = power * jnp.where((owner_dom & (1 << bit)) != 0, 2.0 ** (1 << bit), 1.0)
    signed = jnp.where(lifted, -power, power)
    key_lane = lane == order + KEY_LANE + part * BLOCK
    own_ref[...] = jnp.where(held & key_lane, signed, 0.0)
    up_ref[...] = jnp.where(lifted & key_lane, power, 0.0)
    down_ref[...] = jnp.where(held & key_lane, -power, 0.0)
    key_ref[...] = jnp.where(valid, signed, 2.0**-40)


def route_shapes(dom_count):
    def table(rows, columns, dtype):
        return jax.ShapeDtypeStruct((rows, columns), dtype)

    full = table(ROWS, LANES, F32)
    return (
        table(ROWS, LANES, BF),
        table(2 * dom_count + BLOCK, ROWS, BF),
        table(2 * BLOCK, ROWS, BF),
        table(GROUP, LANES, F32),
        full,
        full,
        full,
        full,
    )


def exact_dot(onehot, values):
    high = values.astype(BF)
    rest = values - high.astype(F32)
    middle = rest.astype(BF)
    low = (rest - middle.astype(F32)).astype(BF)
    total = jnp.dot(onehot, high, preferred_element_type=F32)
    total = total + jnp.dot(onehot, middle, preferred_element_type=F32)
    return total + jnp.dot(onehot, low, preferred_element_type=F32)


def transposed(left, right):
    return lax.dot_general(left, right, (((1,), (1,)), ((), ())), preferred_element_type=F32)


def condense_kernel(dom_count, *refs):
    sources, small, outputs = refs[:4], refs[4:8], refs[8:18]
    schur_ref, condensed_ref = outputs[:2]
    inverse, stacked, back, diagonal, interior, boundary, owner, slot, rows, ends, sems, small_sems, owners, slots = refs[18:]
    elements, width = diagonal.shape[:2]
    small_copies = [
        pltpu.make_async_copy(source, target, small_sems.at[i])
        for i, (source, target) in enumerate(zip(small, (interior, boundary, owner, slot)))
    ]

    def copies(e):
        targets = (inverse.at[e], stacked.at[e, pl.ds(0, width)], back.at[e], diagonal.at[e])
        return [
            pltpu.make_async_copy(source.at[e], target, sems.at[e, i])
            for i, (source, target) in enumerate(zip(sources, targets))
        ]

    for copy in small_copies:
        copy.start()

    @pl.loop(0, elements)
    def _(e):
        for copy in copies(e):
            copy.start()

    for copy in small_copies:
        copy.wait()
    fill_routes(dom_count, owner, slot, *outputs[2:], owners, slots)
    condensed_ref[...] = jnp.zeros(condensed_ref.shape, F32)
    rows[:elements] = interior[...].astype(F32)
    ends[:elements] = boundary[...].astype(F32)

    @pl.loop(0, elements)
    def _(e):
        right = jnp.broadcast_to(rows[pl.ds(e, 1), :], (BLOCK, rows.shape[1]))
        stacked[e, width:] = right.astype(BF)
        for copy in copies(e):
            copy.wait()
        coupled = transposed(stacked[e], inverse[e]).astype(BF)
        product = transposed(coupled, back[e])
        schur_ref[e] = (diagonal[e].astype(F32).T - product[:width]).astype(BF)
        condensed = ends[pl.ds(e, 1), :] - product[width : width + 1]
        condensed_ref[pl.ds(e, 1), :] = condensed.astype(BF).astype(F32)


def condense(dom_count, blocks, small):
    elements, inner, _ = blocks[0].shape
    width = blocks[3].shape[1]

    def kernel(*refs):
        condense_kernel(dom_count, *refs)

    big = [pltpu.VMEM(array.shape, BF) for array in blocks]
    big[1] = pltpu.VMEM((elements, width + BLOCK, inner), BF)
    flops = 2 * elements * (inner * inner * width + inner * width * width)
    return pl.pallas_call(
        kernel,
        in_specs=[pl.BlockSpec(memory_space=pltpu.HBM)] * (len(blocks) + len(small)),
        out_shape=(
            jax.ShapeDtypeStruct((elements, width, width), BF),
            jax.ShapeDtypeStruct((GROUP, width), F32),
        )
        + route_shapes(dom_count),
        scratch_shapes=big
        + [pltpu.VMEM(array.shape, array.dtype) for array in small]
        + [
            pltpu.VMEM((GROUP, inner), F32),
            pltpu.VMEM((GROUP, width), F32),
            pltpu.SemaphoreType.DMA((elements, 4)),
            pltpu.SemaphoreType.DMA((4,)),
            pltpu.VMEM((GROUP, LANES), jnp.int32),
            pltpu.VMEM((GROUP, LANES), jnp.int32),
        ],
        compiler_params=params(28),
        cost_estimate=pl.CostEstimate(flops=flops, bytes_accessed=15_000_000, transcendentals=0),
        name="condense",
    )(*in_hbm(*blocks, *small))


def products(vectors, schur_ref):
    terms = jnp.zeros(vectors.shape, F32)
    for e in range(schur_ref.shape[0]):
        part = jnp.dot(vectors, schur_ref[e], preferred_element_type=F32)
        terms = jnp.where(iota(terms.shape, 0) == e, part, terms)
    return terms


def gather_wide(values, wide, face_width):
    for k in range(SIDES):
        wide[:, k * face_width : (k + 1) * face_width] = values[k * GROUP : (k + 1) * GROUP, :face_width]
    return wide[...].astype(BF)


def split_rows(wide, tall, face_width):
    tall[...] = jnp.zeros(tall.shape, F32)
    for k in range(SIDES):
        tall[k * GROUP : (k + 1) * GROUP, :face_width] = wide[:, k * face_width : (k + 1) * face_width]
    return tall[...]


def first_kernel(
    face_width,
    here_ref,
    above_ref,
    schur_ref,
    condensed_ref,
    pick_ref,
    compact_ref,
    own_ref,
    up_ref,
    down_ref,
    key_ref,
    own_out,
    up_out,
    down_out,
    terms_out,
    key_out,
    wide,
    tall,
):
    table = jnp.concatenate([here_ref[...], above_ref[...]], axis=0)
    values = jnp.dot(pick_ref[...], table, preferred_element_type=F32)
    face = 16.0 + jnp.broadcast_to(values[:, FACE_LANE : FACE_LANE + 1], values.shape)
    vectors = gather_wide(values, wide, face_width)
    wide[...] = products(vectors, schur_ref) - condensed_ref[...]
    rows = split_rows(wide, tall, face_width)
    terms_out[...] = rows
    key_out[...] = face * key_ref[...]
    packed = jnp.dot(compact_ref[...], rows.astype(BF), preferred_element_type=F32)
    held = packed[:BLOCK]
    lifted = packed[BLOCK:]
    lane = iota((BLOCK, LANES), 1)
    line = iota((BLOCK, LANES), 0)

    def key_row(ref, index):
        return jnp.where(line == index, jnp.sum(face * ref[...], axis=0, keepdims=True), 0.0)

    def main(block, far):
        return pltpu.roll(jnp.where(lane < KEY_LANE, block, 0.0), KEY_LANE if far else 0, axis=1)

    def tail(block, index):
        ends = (lane >= KEY_LANE) & (lane < face_width)
        return pltpu.roll(jnp.where(ends, block, 0.0), (LANES - KEY_LANE + index * BLOCK) % LANES, axis=1)

    own_out[:BLOCK] = main(held, False).astype(BF)
    own_out[BLOCK : 2 * BLOCK] = main(lifted, False).astype(BF)
    own_out[2 * BLOCK :] = (
        tail(held, 0) + tail(lifted, 1) + key_row(own_ref, 0) - key_row(up_ref, 1)
    ).astype(BF)
    up_out[:BLOCK] = main(lifted, True).astype(BF)
    up_out[BLOCK:] = (tail(lifted, 2) + key_row(up_ref, 2)).astype(BF)
    down_out[:BLOCK] = main(held, True).astype(BF)
    down_out[BLOCK:] = (tail(held, 3) + key_row(down_ref, 3)).astype(BF)


def first_terms(face_width, *arrays):
    width = arrays[2].shape[1]

    def kernel(*refs):
        first_kernel(face_width, *refs)

    return pl.pallas_call(
        kernel,
        out_shape=(
            jax.ShapeDtypeStruct((3 * BLOCK, LANES), BF),
            jax.ShapeDtypeStruct((2 * BLOCK, LANES), BF),
            jax.ShapeDtypeStruct((2 * BLOCK, LANES), BF),
            jax.ShapeDtypeStruct((ROWS, LANES), F32),
            jax.ShapeDtypeStruct((ROWS, LANES), F32),
        ),
        scratch_shapes=[pltpu.VMEM((GROUP, width), F32), pltpu.VMEM((ROWS, LANES), F32)],
        compiler_params=params(),
        name="first_terms",
    )(*arrays)


def pack_kernel(own_ref, below_ref, above_ref, out_ref):
    own = own_ref[...].astype(F32)
    below = below_ref[...].astype(F32)
    above = above_ref[...].astype(F32)
    start = own[:BLOCK] + below[:BLOCK]
    middle = own[BLOCK : 2 * BLOCK] + above[:BLOCK]
    ends = own[2 * BLOCK :] + below[BLOCK:] + above[BLOCK:]
    rows = jnp.concatenate([start, middle, ends], axis=0).astype(BF)
    for d in range(out_ref.shape[0]):
        out_ref[d] = rows


def pack(dom_count, own, below, above):
    return pl.pallas_call(
        pack_kernel,
        out_shape=jax.ShapeDtypeStruct((dom_count,) + own.shape, BF),
        compiler_params=params(4),
        name="pack",
    )(own, below, above)


def second_kernel(
    face_width, slab_ref, terms_ref, key_ref, schur_ref, put_ref, code_ref, held_out, lifted_out, wide, tall
):
    devices = slab_ref.shape[0]
    depth = devices * BLOCK
    chunks = depth // LANES
    start = slab_ref[:, :BLOCK, :].reshape(depth, LANES)
    middle = slab_ref[:, BLOCK : 2 * BLOCK, :].reshape(depth, LANES)
    ends = slab_ref[:, 2 * BLOCK :, :].reshape(depth, LANES)
    count = 4 * chunks
    shape = (2 * count, depth)
    line = iota(shape, 0)
    half = lax.div(line, count)
    block = lax.div(lax.rem(line, count), chunks)
    chunk = lax.rem(line, chunks)
    column = iota(shape, 1)
    chosen = (lax.rem(column, BLOCK) == block) & (lax.div(column, LANES // 2) == 2 * chunk + half)
    found = jnp.dot(jnp.where(chosen, 1.0, 0.0).astype(BF), ends, preferred_element_type=F32)
    lane = iota((count, LANES), 1)
    keys = jnp.where(lane < KEY_LANE, pltpu.roll(found[:count], KEY_LANE, axis=1), found[count:])
    key = key_ref[...]

    def match(b):
        return jnp.concatenate(
            [jnp.where(key == keys[b * chunks + c : b * chunks + c + 1], 1.0, 0.0).astype(BF) for c in range(chunks)],
            axis=1,
        )

    matches = [match(b) for b in range(4)]
    outer = jnp.dot(jnp.concatenate([matches[0], matches[2]], axis=0), start, preferred_element_type=F32)
    inner = jnp.dot(jnp.concatenate([matches[1], matches[3]], axis=0), middle, preferred_element_type=F32)
    last = jnp.dot(jnp.concatenate(matches, axis=0), ends, preferred_element_type=F32)
    lane = iota((ROWS, LANES), 1)
    near = outer[:ROWS] + inner[:ROWS]
    far = outer[ROWS:] + inner[ROWS:]
    both = jnp.where(lane < KEY_LANE, near + pltpu.roll(far, KEY_LANE, axis=1), 0.0)
    for b in range(4):
        moved = pltpu.roll(last[b * ROWS : (b + 1) * ROWS], KEY_LANE - b * BLOCK, axis=1)
        both = both + jnp.where((lane >= KEY_LANE) & (lane < face_width), moved, 0.0)
    first = terms_ref[...]
    residual = both + (first - first.astype(BF).astype(F32))
    vectors = gather_wide(residual, wide, face_width)
    wide[...] = products(vectors, schur_ref)
    second = split_rows(wide, tall, face_width)
    pair = jnp.concatenate([first, second], axis=1)
    placed = exact_dot(put_ref[...], pair)
    positions = held_out.shape[0]
    held_out[...] = placed[:positions]
    codes = jnp.concatenate([code_ref[...], code_ref[...]], axis=1)[:1]
    lifted_out[...] = jnp.where(iota(lifted_out.shape, 0) == BLOCK - 1, codes, placed[positions:])


def second_terms(face_width, positions, *arrays):
    width = arrays[3].shape[1]

    def kernel(*refs):
        second_kernel(face_width, *refs)

    return pl.pallas_call(
        kernel,
        out_shape=(
            jax.ShapeDtypeStruct((positions, 2 * LANES), F32),
            jax.ShapeDtypeStruct((BLOCK, 2 * LANES), F32),
        ),
        scratch_shapes=[pltpu.VMEM((GROUP, width), F32), pltpu.VMEM((ROWS, LANES), F32)],
        compiler_params=params(),
        name="second_terms",
    )(*arrays)


def merge_kernel(held_ref, raised_ref, out_ref):
    raised = raised_ref[...]
    code = raised[BLOCK - 1 :, :BLOCK]
    place = iota((out_ref.shape[0], BLOCK), 0).astype(F32)
    onehot = jnp.where(place == code, 1.0, 0.0)
    out_ref[...] = held_ref[...] + exact_dot(onehot.astype(BF), raised)


def merge(held, raised):
    return pl.pallas_call(
        merge_kernel,
        out_shape=jax.ShapeDtypeStruct(held.shape, F32),
        compiler_params=params(4),
        name="merge",
    )(held, raised)


def collect_kernel(arrived_ref, slots_ref, residual_ref, image_ref, slots):
    faces, width = residual_ref.shape
    onehot = face_onehot(slots_ref, slots, arrived_ref.shape[0])
    total = lax.dot_general(
        onehot, arrived_ref[...], (((0,), (0,)), ((), ())), preferred_element_type=F32, precision=EXACT
    )
    residual_ref[...] = total[:faces, :width]
    image_ref[...] = total[:faces, LANES : LANES + width]


def collect(arrived, slots, faces, width):
    out = jax.ShapeDtypeStruct((faces, width), F32)
    return pl.pallas_call(
        collect_kernel,
        out_shape=(out, out),
        scratch_shapes=[pltpu.VMEM((2, BLOCK), jnp.int32)],
        compiler_params=params(4),
        name="collect",
    )(arrived, slots)


def on_device(
    local_inverse,
    local_trace,
    trace_local,
    trace_trace,
    local_rhs,
    trace_rhs,
    trace_state,
    side_owner,
    side_slot,
    face_slots,
):
    dom_count = lax.axis_size("dom")
    faces, face_width = trace_state.shape
    positions = 2 * dom_count
    slots = face_slots.T
    blocks = (local_inverse, jnp.swapaxes(local_trace, 1, 2), trace_local, trace_trace)
    outgoing = spread(slots, trace_state, positions)
    here = exchange(outgoing.reshape(dom_count, 2, LANES)).reshape(positions, LANES)
    schur, condensed, pick, put, compact, codes, own_keys, up_keys, down_keys, keys = condense(
        dom_count, blocks, (local_rhs, trace_rhs, side_owner, side_slot)
    )
    here, schur = lax.optimization_barrier((here, schur))
    above = shift(here, -1)
    own, lifted, held, terms, key = first_terms(
        face_width,
        here,
        above,
        schur,
        condensed,
        pick,
        compact,
        own_keys,
        up_keys,
        down_keys,
        keys,
    )
    slab = exchange(pack(dom_count, own, shift(lifted, 1), shift(held, -1)))
    stay, rise = second_terms(face_width, positions, slab, terms, key, schur, put, codes)
    arriving = merge(stay, shift(rise, 1))
    arrived = exchange(arriving.reshape(dom_count, 2, 2 * LANES)).reshape(positions, 2 * LANES)
    return collect(arrived, slots, faces, face_width)


def solution(mesh):
    both = ("grp", "dom")
    blocks = (P(both, None, None),) * 4
    rows = (P(both, None),) * 6
    return jax.shard_map(
        on_device,
        mesh=mesh,
        in_specs=blocks + rows,
        out_specs=(P(both, None), P(both, None)),
        check_vma=False,
    )
```

```python
import jax
import jax.numpy as jnp
from jax import lax
from jax.experimental import pallas as pl
from jax.experimental.pallas import tpu as pltpu
from jax.sharding import PartitionSpec as P

BF = jnp.bfloat16
F32 = jnp.float32
LANES = 128
SIDES = 6
GROUP = 8
ROWS = SIDES * GROUP
BLOCK = 16
FACE_LANE = 80
KEY_LANE = 64
WIDE = 16
PACKED = 40


def iota(shape, dim):
    return lax.broadcasted_iota(jnp.int32, shape, dim)


def params(mib=12):
    return pltpu.CompilerParams(vmem_limit_bytes=mib * 1024 * 1024)


def in_hbm(*arrays):
    return [pltpu.with_memory_space_constraint(array, pltpu.HBM) for array in arrays]


def shift(payload, by):
    devices = lax.axis_size("grp")
    return lax.ppermute(payload, "grp", [(i, (i + by) % devices) for i in range(devices)])


def exchange(payload):
    return lax.all_to_all(payload, "dom", split_axis=0, concat_axis=0, tiled=True)


def face_onehot(slots_ref, scratch, positions):
    scratch[...] = jnp.full(scratch.shape, -1, jnp.int32)
    scratch[:, : slots_ref.shape[1]] = slots_ref[...]
    place = iota((positions, BLOCK), 0)
    hit = (place == scratch[0:1, :]) | (place == scratch[1:2, :])
    return jnp.where(hit, 1.0, 0.0)


def spread_kernel(slots_from, state_from, out_ref, slots_ref, state_ref, slots, rows, sems):
    copies = [
        pltpu.make_async_copy(slots_from, slots_ref, sems.at[0]),
        pltpu.make_async_copy(state_from, state_ref, sems.at[1]),
    ]
    for copy in copies:
        copy.start()
    for copy in copies:
        copy.wait()
    faces, width = state_ref.shape
    rows[...] = jnp.zeros(rows.shape, F32)
    rows[:faces, :width] = state_ref[...].astype(F32)
    lane = iota(rows.shape, 1)
    index = iota(rows.shape, 0).astype(F32)
    table = jnp.where(lane == FACE_LANE, index, rows[...]).astype(BF)
    onehot = face_onehot(slots_ref, slots, out_ref.shape[0]).astype(BF)
    out_ref[...] = jnp.dot(onehot, table, preferred_element_type=F32).astype(BF)


def spread(slots, state, positions):
    return pl.pallas_call(
        spread_kernel,
        in_specs=[pl.BlockSpec(memory_space=pltpu.HBM)] * 2,
        out_shape=jax.ShapeDtypeStruct((positions, LANES), BF),
        scratch_shapes=[
            pltpu.VMEM(slots.shape, slots.dtype),
            pltpu.VMEM(state.shape, state.dtype),
            pltpu.VMEM((2, BLOCK), jnp.int32),
            pltpu.VMEM((BLOCK, LANES), F32),
            pltpu.SemaphoreType.DMA((2,)),
        ],
        compiler_params=params(4),
        name="spread",
    )(*in_hbm(slots, state))


def fill_routes(
    dom_count, owner_ref, slot_ref, pick_ref, put_ref, compact_ref, code_ref, own_ref, up_ref, down_ref, key_ref, owners, slots
):
    elements = owner_ref.shape[0]
    owners[...] = jnp.full(owners.shape, -1, jnp.int32)
    slots[...] = jnp.zeros(slots.shape, jnp.int32)
    owners[:elements, :SIDES] = owner_ref[...]
    slots[:elements, :SIDES] = slot_ref[...]

    def rows(ref):
        return jnp.concatenate([jnp.broadcast_to(ref[:, k : k + 1], (GROUP, LANES)) for k in range(SIDES)], axis=0)

    owner = rows(owners)
    slot = rows(slots)
    grp = lax.axis_index("grp")
    part = lax.axis_index("dom") % 4
    valid = owner >= 0
    owner = jnp.maximum(owner, 0)
    owner_dom = lax.rem(owner, dom_count)
    owner_grp = lax.div(owner, dom_count)
    lifted = valid & (owner_grp != grp)
    held = valid & (owner_grp == grp)
    lane = iota((ROWS, LANES), 1)
    place = owner_dom * 2 + slot
    pick = jnp.where(valid & (lane == place + jnp.where(lifted, 2 * dom_count, 0)), 1.0, 0.0)
    pick_ref[...] = pick.astype(BF)
    pad = jnp.zeros((LANES - ROWS, LANES), F32)
    put_ref[: 2 * dom_count] = jnp.concatenate([pick, pad], axis=0).T[: 2 * dom_count, :ROWS].astype(BF)
    before = jnp.where(iota((ROWS, ROWS), 1) < iota((ROWS, ROWS), 0), 1.0, 0.0).astype(BF)

    def rank(flag):
        counts = jnp.dot(before, jnp.where(flag, 1.0, 0.0).astype(BF), preferred_element_type=F32)
        return counts.astype(jnp.int32)

    order = jnp.where(lifted, rank(lifted), rank(held))
    seat = valid & (lane == order + jnp.where(lifted, BLOCK, 0))
    compact = jnp.concatenate([jnp.where(seat, 1.0, 0.0), pad], axis=0).T
    compact_ref[...] = compact[: 2 * BLOCK, :ROWS].astype(BF)
    put_ref[2 * dom_count :] = compact[BLOCK : 2 * BLOCK, :ROWS].astype(BF)
    code = jnp.where(lifted & (lane == order), place.astype(F32) + 1.0, 0.0)
    code_ref[...] = jnp.broadcast_to(jnp.sum(code, axis=0, keepdims=True) - 1.0, code_ref.shape)
    power = jnp.full((ROWS, LANES), 2.0**-16, F32)
    for bit in range(5):
        power = power * jnp.where((owner_dom & (1 << bit)) != 0, 2.0 ** (1 << bit), 1.0)
    signed = jnp.where(lifted, -power, power)
    key_lane = lane == order + KEY_LANE + part * BLOCK
    own_ref[...] = jnp.where(held & (lane == order + part * BLOCK), signed, 0.0)
    up_ref[...] = jnp.where(lifted & key_lane, power, 0.0)
    down_ref[...] = jnp.where(held & key_lane, -power, 0.0)
    key_ref[...] = jnp.where(valid, signed, 2.0**-40)


def route_shapes(dom_count):
    def table(rows, columns, dtype):
        return jax.ShapeDtypeStruct((rows, columns), dtype)

    full = table(ROWS, LANES, F32)
    return (
        table(ROWS, LANES, BF),
        table(2 * dom_count + BLOCK, ROWS, BF),
        table(2 * BLOCK, ROWS, BF),
        table(GROUP, LANES, F32),
        full,
        full,
        full,
        full,
    )


def exact_dot(onehot, values):
    high = values.astype(BF)
    rest = values - high.astype(F32)
    middle = rest.astype(BF)
    low = (rest - middle.astype(F32)).astype(BF)
    total = jnp.dot(onehot, high, preferred_element_type=F32)
    total = total + jnp.dot(onehot, middle, preferred_element_type=F32)
    return total + jnp.dot(onehot, low, preferred_element_type=F32)


def transposed(left, right):
    return lax.dot_general(left, right, (((1,), (1,)), ((), ())), preferred_element_type=F32)


def condense_kernel(first, dom_count, *refs):
    sources, refs = refs[:4], refs[4:]
    small, refs = (refs[:4], refs[4:]) if first == 0 else (refs[:2], refs[2:])
    schur_ref, condensed_ref = refs[:2]
    tables = refs[2:10] if first == 0 else ()
    inverse, stacked, back, diagonal, rows, ends, sems, small_sems, *arrived = refs[2 + len(tables) :]
    routing = arrived[len(small) :]
    arrived = arrived[: len(small)]
    count, width = diagonal.shape[:2]
    elements = small[0].shape[0]
    small_copies = [
        pltpu.make_async_copy(source, target, small_sems.at[i]) for i, (source, target) in enumerate(zip(small, arrived))
    ]

    def copies(e):
        targets = (inverse.at[e], stacked.at[e, pl.ds(0, width)], back.at[e], diagonal.at[e])
        return [
            pltpu.make_async_copy(source.at[first + e], target, sems.at[e, i])
            for i, (source, target) in enumerate(zip(sources, targets))
        ]

    for copy in small_copies:
        copy.start()

    @pl.loop(0, count)
    def _(e):
        for copy in copies(e):
            copy.start()

    for copy in small_copies:
        copy.wait()
    if first == 0:
        fill_routes(dom_count, arrived[2], arrived[3], *tables, *routing)
    condensed_ref[...] = jnp.zeros(condensed_ref.shape, F32)
    rows[:elements] = arrived[0][...].astype(F32)
    ends[:elements] = arrived[1][...].astype(F32)

    def element(e, step):
        row = pl.ds(first + e, 1)
        right = jnp.broadcast_to(rows[row, :], (BLOCK, rows.shape[1]))
        stacked[e, width:] = right.astype(BF)
        waits = copies(e)
        for copy in waits[:step]:
            copy.wait()
        coupled = transposed(stacked[e], inverse[e]).astype(BF)
        for copy in waits[step:]:
            copy.wait()
        product = transposed(coupled, back[e])
        schur_ref[e] = (diagonal[e].astype(F32).T - product[:width]).astype(BF)
        condensed = ends[row, :] - product[width : width + 1]
        condensed_ref[row, :] = condensed.astype(BF).astype(F32)

    element(0, 2)
    if count > 1:
        pl.loop(1, count)(lambda e: element(e, 4))


def condense(first, count, dom_count, blocks, small):
    inner = blocks[0].shape[1]
    width = blocks[3].shape[1]

    def kernel(*refs):
        condense_kernel(first, dom_count, *refs)

    out_shape = (
        jax.ShapeDtypeStruct((count, width, width), BF),
        jax.ShapeDtypeStruct((GROUP, width), F32),
    )
    shapes = ((count, inner, inner), (count, width + BLOCK, inner), (count, width, inner), (count, width, width))
    scratch = [pltpu.VMEM(shape, BF) for shape in shapes]
    scratch += [pltpu.VMEM((GROUP, inner), F32), pltpu.VMEM((GROUP, width), F32)]
    scratch += [pltpu.SemaphoreType.DMA((count, 4)), pltpu.SemaphoreType.DMA((len(small),))]
    scratch += [pltpu.VMEM(array.shape, array.dtype) for array in small]
    if first == 0:
        out_shape += route_shapes(dom_count)
        scratch += [pltpu.VMEM((GROUP, LANES), jnp.int32)] * 2
    flops = 2 * count * (inner * inner * width + inner * width * width)
    return pl.pallas_call(
        kernel,
        in_specs=[pl.BlockSpec(memory_space=pltpu.HBM)] * (len(blocks) + len(small)),
        out_shape=out_shape,
        scratch_shapes=scratch,
        compiler_params=params(24),
        cost_estimate=pl.CostEstimate(flops=flops, bytes_accessed=count * 3_000_000, transcendentals=0),
        name="condense",
    )(*in_hbm(*blocks, *small))


def products(vectors, schur_refs):
    terms = jnp.zeros(vectors.shape, F32)
    element = 0
    for schur_ref in schur_refs:
        for e in range(schur_ref.shape[0]):
            part = jnp.dot(vectors, schur_ref[e], preferred_element_type=F32)
            terms = jnp.where(iota(terms.shape, 0) == element, part, terms)
            element += 1
    return terms


def gather_wide(values, wide, face_width):
    for k in range(SIDES):
        wide[:, k * face_width : (k + 1) * face_width] = values[k * GROUP : (k + 1) * GROUP, :face_width]
    return wide[...].astype(BF)


def split_rows(wide, tall, face_width):
    tall[...] = jnp.zeros(tall.shape, F32)
    for k in range(SIDES):
        tall[k * GROUP : (k + 1) * GROUP, :face_width] = wide[:, k * face_width : (k + 1) * face_width]
    return tall[...]


def first_kernel(
    face_width,
    here_ref,
    above_ref,
    schur_a,
    schur_b,
    condensed_a,
    condensed_b,
    pick_ref,
    compact_ref,
    own_ref,
    up_ref,
    down_ref,
    key_ref,
    own_out,
    up_out,
    down_out,
    terms_out,
    key_out,
    wide,
    tall,
):
    table = jnp.concatenate([here_ref[...], above_ref[...]], axis=0)
    values = jnp.dot(pick_ref[...], table, preferred_element_type=F32)
    face = 16.0 + jnp.broadcast_to(values[:, FACE_LANE : FACE_LANE + 1], values.shape)
    vectors = gather_wide(values, wide, face_width)
    wide[...] = products(vectors, (schur_a, schur_b)) - (condensed_a[...] + condensed_b[...])
    rows = split_rows(wide, tall, face_width)
    terms_out[...] = rows
    key_out[...] = face * key_ref[...]
    packed = jnp.dot(compact_ref[...], rows.astype(BF), preferred_element_type=F32)
    held = packed[:BLOCK]
    lifted = packed[BLOCK:]
    lane = iota((BLOCK, LANES), 1)
    line = iota((BLOCK, LANES), 0)

    def key_row(ref, index):
        return jnp.where(line == index, jnp.sum(face * ref[...], axis=0, keepdims=True), 0.0)

    def main(block, far):
        return pltpu.roll(jnp.where(lane < KEY_LANE, block, 0.0), KEY_LANE if far else 0, axis=1)

    def tail(block, index):
        ends = jnp.where((lane >= KEY_LANE) & (lane < face_width), block, 0.0)
        place = LANES - KEY_LANE + 2 * index * WIDE
        upper = pltpu.roll(ends[:GROUP], place % LANES, axis=1)
        return upper + pltpu.roll(ends[GROUP:], (place + WIDE) % LANES, axis=1)

    up_keys = key_row(up_ref, BLOCK - 1)
    own_out[:BLOCK] = (main(held, False) + key_row(own_ref, BLOCK - 1)).astype(BF)
    own_out[BLOCK : 2 * BLOCK] = (main(lifted, False) - pltpu.roll(up_keys, KEY_LANE, axis=1)).astype(BF)
    none = jnp.zeros((GROUP, LANES), F32)
    own_out[2 * BLOCK :] = jnp.concatenate([tail(held, 0) + tail(lifted, 1), none], axis=0).astype(BF)
    up_out[:BLOCK] = (main(lifted, True) + up_keys).astype(BF)
    up_out[BLOCK:] = jnp.concatenate([tail(lifted, 2), none], axis=0).astype(BF)
    down_out[:BLOCK] = (main(held, True) + key_row(down_ref, BLOCK - 1)).astype(BF)
    down_out[BLOCK:] = jnp.concatenate([tail(held, 3), none], axis=0).astype(BF)


def first_terms(face_width, *arrays):
    width = arrays[2].shape[1]

    def kernel(*refs):
        first_kernel(face_width, *refs)

    return pl.pallas_call(
        kernel,
        out_shape=(
            jax.ShapeDtypeStruct((3 * BLOCK, LANES), BF),
            jax.ShapeDtypeStruct((2 * BLOCK, LANES), BF),
            jax.ShapeDtypeStruct((2 * BLOCK, LANES), BF),
            jax.ShapeDtypeStruct((ROWS, LANES), F32),
            jax.ShapeDtypeStruct((ROWS, LANES), F32),
        ),
        scratch_shapes=[pltpu.VMEM((GROUP, width), F32), pltpu.VMEM((ROWS, LANES), F32)],
        compiler_params=params(),
        name="first_terms",
    )(*arrays)


def pack_kernel(own_ref, below_ref, above_ref, out_ref):
    own = own_ref[...].astype(F32)
    below = below_ref[...].astype(F32)
    above = above_ref[...].astype(F32)
    start = own[:BLOCK] + below[:BLOCK]
    middle = own[BLOCK : 2 * BLOCK] + above[:BLOCK]
    ends = own[2 * BLOCK :] + below[BLOCK:] + above[BLOCK:]
    rows = jnp.concatenate([start, middle, ends[:GROUP]], axis=0).astype(BF)
    for d in range(out_ref.shape[0]):
        out_ref[d] = rows


def pack(dom_count, own, below, above):
    return pl.pallas_call(
        pack_kernel,
        out_shape=jax.ShapeDtypeStruct((dom_count, PACKED, LANES), BF),
        compiler_params=params(4),
        name="pack",
    )(own, below, above)


def second_kernel(
    face_width, slab_ref, terms_ref, key_ref, schur_a, schur_b, put_ref, code_ref, held_out, lifted_out, wide, tall
):
    devices = slab_ref.shape[0]
    depth = devices * BLOCK
    chunks = depth // LANES
    start = slab_ref[:, :BLOCK, :].reshape(depth, LANES)
    middle = slab_ref[:, BLOCK : 2 * BLOCK, :].reshape(depth, LANES)
    ends = slab_ref[:, 2 * BLOCK :, :].astype(F32)
    ends = jnp.concatenate([ends, ends], axis=1).reshape(depth, LANES)
    upper = lax.rem(lax.div(iota((depth, LANES), 1), WIDE), 2) == lax.div(lax.rem(iota((depth, LANES), 0), BLOCK), GROUP)
    ends = jnp.where(upper, ends, 0.0).astype(BF)
    shape = (2 * GROUP, depth)
    half = lax.div(iota(shape, 0), GROUP)
    chunk = lax.rem(iota(shape, 0), GROUP)
    column = iota(shape, 1)
    chosen = (lax.rem(column, BLOCK) == BLOCK - 1) & (lax.div(column, LANES // 2) == 2 * chunk + half)
    chosen = jnp.where(chosen, 1.0, 0.0).astype(BF)
    lane = iota((GROUP, LANES), 1)
    key = key_ref[...]

    def block_keys(rows):
        found = jnp.dot(chosen, rows, preferred_element_type=F32)
        low, high = found[:GROUP], found[GROUP:]
        near = jnp.where(lane < KEY_LANE, low, pltpu.roll(high, KEY_LANE, axis=1))
        far = jnp.where(lane < KEY_LANE, pltpu.roll(low, KEY_LANE, axis=1), high)
        return near, far

    outer_keys = block_keys(start)
    inner_keys = block_keys(middle)
    keys = (outer_keys[0], inner_keys[0], outer_keys[1], inner_keys[1])

    def match(b):
        return jnp.concatenate(
            [jnp.where(key == keys[b][c : c + 1], 1.0, 0.0).astype(BF) for c in range(chunks)], axis=1
        )

    matches = [match(b) for b in range(4)]
    outer = jnp.dot(jnp.concatenate([matches[0], matches[2]], axis=0), start, preferred_element_type=F32)
    inner = jnp.dot(jnp.concatenate([matches[1], matches[3]], axis=0), middle, preferred_element_type=F32)
    last = jnp.dot(jnp.concatenate(matches, axis=0), ends, preferred_element_type=F32)
    lane = iota((ROWS, LANES), 1)
    near = outer[:ROWS] + inner[:ROWS]
    far = outer[ROWS:] + inner[ROWS:]
    both = jnp.where(lane < KEY_LANE, near + pltpu.roll(far, KEY_LANE, axis=1), 0.0)
    for b in range(4):
        line = last[b * ROWS : (b + 1) * ROWS]
        place = LANES + KEY_LANE - 2 * b * WIDE
        moved = pltpu.roll(line, place % LANES, axis=1) + pltpu.roll(line, (place - WIDE) % LANES, axis=1)
        both = both + jnp.where((lane >= KEY_LANE) & (lane < face_width), moved, 0.0)
    first = terms_ref[...]
    residual = both + (first - first.astype(BF).astype(F32))
    vectors = gather_wide(residual, wide, face_width)
    wide[...] = products(vectors, (schur_a, schur_b))
    second = split_rows(wide, tall, face_width)
    pair = jnp.concatenate([first, second], axis=1)
    placed = exact_dot(put_ref[...], pair)
    positions = held_out.shape[0]
    held_out[...] = placed[:positions]
    codes = jnp.concatenate([code_ref[...], code_ref[...]], axis=1)[:1]
    lifted_out[...] = jnp.where(iota(lifted_out.shape, 0) == BLOCK - 1, codes, placed[positions:])


def second_terms(face_width, positions, *arrays):
    width = arrays[3].shape[1]

    def kernel(*refs):
        second_kernel(face_width, *refs)

    return pl.pallas_call(
        kernel,
        out_shape=(
            jax.ShapeDtypeStruct((positions, 2 * LANES), F32),
            jax.ShapeDtypeStruct((BLOCK, 2 * LANES), F32),
        ),
        scratch_shapes=[pltpu.VMEM((GROUP, width), F32), pltpu.VMEM((ROWS, LANES), F32)],
        compiler_params=params(),
        name="second_terms",
    )(*arrays)


def merge_kernel(held_ref, raised_ref, out_ref):
    raised = raised_ref[...]
    code = raised[BLOCK - 1 :, :BLOCK]
    place = iota((out_ref.shape[0], BLOCK), 0).astype(F32)
    onehot = jnp.where(place == code, 1.0, 0.0)
    out_ref[...] = held_ref[...] + exact_dot(onehot.astype(BF), raised)


def merge(held, raised):
    return pl.pallas_call(
        merge_kernel,
        out_shape=jax.ShapeDtypeStruct(held.shape, F32),
        compiler_params=params(4),
        name="merge",
    )(held, raised)


def collect_kernel(arrived_ref, slots_ref, residual_ref, image_ref, slots):
    faces, width = residual_ref.shape
    onehot = face_onehot(slots_ref, slots, arrived_ref.shape[0])
    onehot = jnp.concatenate([onehot, jnp.zeros((onehot.shape[0], LANES - BLOCK), F32)], axis=1)
    total = exact_dot(onehot.T[:BLOCK].astype(BF), arrived_ref[...])
    residual_ref[...] = total[:faces, :width]
    image_ref[...] = total[:faces, LANES : LANES + width]


def collect(arrived, slots, faces, width):
    out = jax.ShapeDtypeStruct((faces, width), F32)
    return pl.pallas_call(
        collect_kernel,
        out_shape=(out, out),
        scratch_shapes=[pltpu.VMEM((2, BLOCK), jnp.int32)],
        compiler_params=params(4),
        name="collect",
    )(arrived, slots)


def on_device(
    local_inverse,
    local_trace,
    trace_local,
    trace_trace,
    local_rhs,
    trace_rhs,
    trace_state,
    side_owner,
    side_slot,
    face_slots,
):
    dom_count = lax.axis_size("dom")
    faces, face_width = trace_state.shape
    positions = 2 * dom_count
    slots = face_slots.T
    blocks = (local_inverse, jnp.swapaxes(local_trace, 1, 2), trace_local, trace_trace)
    outgoing = spread(slots, trace_state, positions)
    here = exchange(outgoing.reshape(dom_count, 2, LANES)).reshape(positions, LANES)
    elements = local_inverse.shape[0]
    early = elements - max(elements // 5, 1)
    schur_a, condensed_a, pick, put, compact, codes, own_keys, up_keys, down_keys, keys = condense(
        0, early, dom_count, blocks, (local_rhs, trace_rhs, side_owner, side_slot)
    )
    here, schur_a, boundary = lax.optimization_barrier((here, schur_a, trace_rhs))
    above = shift(here, -1)
    schur_b, condensed_b = condense(early, elements - early, dom_count, blocks, (local_rhs, boundary))
    own, lifted, held, terms, key = first_terms(
        face_width,
        here,
        above,
        schur_a,
        schur_b,
        condensed_a,
        condensed_b,
        pick,
        compact,
        own_keys,
        up_keys,
        down_keys,
        keys,
    )
    slab = exchange(pack(dom_count, own, shift(lifted, 1), shift(held, -1)))
    stay, rise = second_terms(face_width, positions, slab, terms, key, schur_a, schur_b, put, codes)
    arriving = merge(stay, shift(rise, 1))
    arrived = exchange(arriving.reshape(dom_count, 2, 2 * LANES)).reshape(positions, 2 * LANES)
    return collect(arrived, slots, faces, face_width)


def solution(mesh):
    both = ("grp", "dom")
    blocks = (P(both, None, None),) * 4
    rows = (P(both, None),) * 6
    return jax.shard_map(
        on_device,
        mesh=mesh,
        in_specs=blocks + rows,
        out_specs=(P(both, None), P(both, None)),
        check_vma=False,
    )
```

```python
import jax
import jax.numpy as jnp
from jax import lax
from jax.experimental import pallas as pl
from jax.experimental.pallas import tpu as pltpu
from jax.sharding import PartitionSpec as P

BF = jnp.bfloat16
F32 = jnp.float32
LANES = 128
SIDES = 6
GROUP = 8
ROWS = SIDES * GROUP
BLOCK = 16
FACE_LANE = 80
KEY_LANE = 64
WIDE = 16
PACKED = 40


def iota(shape, dim):
    return lax.broadcasted_iota(jnp.int32, shape, dim)


def params(mib=12):
    return pltpu.CompilerParams(vmem_limit_bytes=mib * 1024 * 1024)


def in_hbm(*arrays):
    return [pltpu.with_memory_space_constraint(array, pltpu.HBM) for array in arrays]


def shift(payload, by):
    devices = lax.axis_size("grp")
    return lax.ppermute(payload, "grp", [(i, (i + by) % devices) for i in range(devices)])


def exchange(payload):
    return lax.all_to_all(payload, "dom", split_axis=0, concat_axis=0, tiled=True)


def face_onehot(slots_ref, scratch, positions):
    scratch[...] = jnp.full(scratch.shape, -1, jnp.int32)
    scratch[:, : slots_ref.shape[1]] = slots_ref[...]
    place = iota((positions, BLOCK), 0)
    hit = (place == scratch[0:1, :]) | (place == scratch[1:2, :])
    return jnp.where(hit, 1.0, 0.0)


def spread_kernel(slots_from, state_from, out_ref, slots_ref, state_ref, slots, rows, sems):
    copies = [
        pltpu.make_async_copy(slots_from, slots_ref, sems.at[0]),
        pltpu.make_async_copy(state_from, state_ref, sems.at[1]),
    ]
    for copy in copies:
        copy.start()
    for copy in copies:
        copy.wait()
    faces, width = state_ref.shape
    rows[...] = jnp.zeros(rows.shape, F32)
    rows[:faces, :width] = state_ref[...].astype(F32)
    lane = iota(rows.shape, 1)
    index = iota(rows.shape, 0).astype(F32)
    table = jnp.where(lane == FACE_LANE, index, rows[...]).astype(BF)
    onehot = face_onehot(slots_ref, slots, out_ref.shape[0]).astype(BF)
    out_ref[...] = jnp.dot(onehot, table, preferred_element_type=F32).astype(BF)


def spread(slots, state, positions):
    return pl.pallas_call(
        spread_kernel,
        in_specs=[pl.BlockSpec(memory_space=pltpu.HBM)] * 2,
        out_shape=jax.ShapeDtypeStruct((positions, LANES), BF),
        scratch_shapes=[
            pltpu.VMEM(slots.shape, slots.dtype),
            pltpu.VMEM(state.shape, state.dtype),
            pltpu.VMEM((2, BLOCK), jnp.int32),
            pltpu.VMEM((BLOCK, LANES), F32),
            pltpu.SemaphoreType.DMA((2,)),
        ],
        compiler_params=params(4),
        name="spread",
    )(*in_hbm(slots, state))


def fill_routes(
    dom_count, owner_ref, slot_ref, pick_ref, put_ref, compact_ref, code_ref, own_ref, up_ref, down_ref, key_ref, owners, slots
):
    elements = owner_ref.shape[0]
    owners[...] = jnp.full(owners.shape, -1, jnp.int32)
    slots[...] = jnp.zeros(slots.shape, jnp.int32)
    owners[:elements, :SIDES] = owner_ref[...]
    slots[:elements, :SIDES] = slot_ref[...]

    def rows(ref):
        return jnp.concatenate([jnp.broadcast_to(ref[:, k : k + 1], (GROUP, LANES)) for k in range(SIDES)], axis=0)

    owner = rows(owners)
    slot = rows(slots)
    grp = lax.axis_index("grp")
    part = lax.axis_index("dom") % 4
    valid = owner >= 0
    owner = jnp.maximum(owner, 0)
    owner_dom = lax.rem(owner, dom_count)
    owner_grp = lax.div(owner, dom_count)
    lifted = valid & (owner_grp != grp)
    held = valid & (owner_grp == grp)
    lane = iota((ROWS, LANES), 1)
    place = owner_dom * 2 + slot
    pick = jnp.where(valid & (lane == place + jnp.where(lifted, 2 * dom_count, 0)), 1.0, 0.0)
    pick_ref[...] = pick.astype(BF)
    pad = jnp.zeros((LANES - ROWS, LANES), F32)
    put_ref[: 2 * dom_count] = jnp.concatenate([pick, pad], axis=0).T[: 2 * dom_count, :ROWS].astype(BF)
    before = jnp.where(iota((ROWS, ROWS), 1) < iota((ROWS, ROWS), 0), 1.0, 0.0).astype(BF)

    def rank(flag):
        counts = jnp.dot(before, jnp.where(flag, 1.0, 0.0).astype(BF), preferred_element_type=F32)
        return counts.astype(jnp.int32)

    order = jnp.where(lifted, rank(lifted), rank(held))
    seat = valid & (lane == order + jnp.where(lifted, BLOCK, 0))
    compact = jnp.concatenate([jnp.where(seat, 1.0, 0.0), pad], axis=0).T
    compact_ref[...] = compact[: 2 * BLOCK, :ROWS].astype(BF)
    put_ref[2 * dom_count :] = compact[BLOCK : 2 * BLOCK, :ROWS].astype(BF)
    code = jnp.where(lifted & (lane == order), place.astype(F32) + 1.0, 0.0)
    code_ref[...] = jnp.broadcast_to(jnp.sum(code, axis=0, keepdims=True) - 1.0, code_ref.shape)
    power = jnp.full((ROWS, LANES), 2.0**-16, F32)
    for bit in range(5):
        power = power * jnp.where((owner_dom & (1 << bit)) != 0, 2.0 ** (1 << bit), 1.0)
    signed = jnp.where(lifted, -power, power)
    key_lane = lane == order + KEY_LANE + part * BLOCK
    own_ref[...] = jnp.where(held & (lane == order + part * BLOCK), signed, 0.0)
    up_ref[...] = jnp.where(lifted & key_lane, power, 0.0)
    down_ref[...] = jnp.where(held & key_lane, -power, 0.0)
    key_ref[...] = jnp.where(valid, signed, 2.0**-40)


def route_shapes(dom_count):
    def table(rows, columns, dtype):
        return jax.ShapeDtypeStruct((rows, columns), dtype)

    full = table(ROWS, LANES, F32)
    return (
        table(ROWS, LANES, BF),
        table(2 * dom_count + BLOCK, ROWS, BF),
        table(2 * BLOCK, ROWS, BF),
        table(GROUP, LANES, F32),
        full,
        full,
        full,
        full,
    )


def exact_dot(onehot, values):
    high = values.astype(BF)
    rest = values - high.astype(F32)
    middle = rest.astype(BF)
    low = (rest - middle.astype(F32)).astype(BF)
    total = jnp.dot(onehot, high, preferred_element_type=F32)
    total = total + jnp.dot(onehot, middle, preferred_element_type=F32)
    return total + jnp.dot(onehot, low, preferred_element_type=F32)


def transposed(left, right):
    return lax.dot_general(left, right, (((1,), (1,)), ((), ())), preferred_element_type=F32)


def condense_kernel(first, count, dom_count, *refs):
    early = first == 0
    sources, refs = refs[:4], refs[4:]
    small, refs = (refs[:4], refs[4:]) if early else (refs[:2], refs[2:])
    done, refs = (None, refs) if early else (refs[0], refs[1:])
    schur_ref, condensed_ref = refs[:2]
    tables = refs[2:10] if early else ()
    inverse, stacked, back, diagonal, rows, ends, sems, small_sems, *arrived = refs[2 + len(tables) :]
    routing = arrived[len(small) :]
    arrived = arrived[: len(small)]
    width = diagonal.shape[1]
    elements = small[0].shape[0]
    wraps = lax.axis_index("grp") == 0
    last = jnp.where(wraps, elements, count) if early else jnp.where(wraps, 0, count)
    small_copies = [
        pltpu.make_async_copy(source, target, small_sems.at[i]) for i, (source, target) in enumerate(zip(small, arrived))
    ]

    def copies(e):
        targets = (inverse.at[e], stacked.at[e, pl.ds(0, width)], back.at[e], diagonal.at[e])
        return [
            pltpu.make_async_copy(source.at[first + e], target, sems.at[e, i])
            for i, (source, target) in enumerate(zip(sources, targets))
        ]

    for copy in small_copies:
        copy.start()

    @pl.loop(0, last)
    def _(e):
        for copy in copies(e):
            copy.start()

    for copy in small_copies:
        copy.wait()
    if early:
        fill_routes(dom_count, arrived[2], arrived[3], *tables, *routing)
    condensed_ref[...] = jnp.zeros(condensed_ref.shape, F32)
    rows[:elements] = arrived[0][...].astype(F32)
    ends[:elements] = arrived[1][...].astype(F32)

    @pl.loop(0, last)
    def _(e):
        row = pl.ds(first + e, 1)
        right = jnp.broadcast_to(rows[row, :], (BLOCK, rows.shape[1]))
        stacked[e, width:] = right.astype(BF)
        for copy in copies(e):
            copy.wait()
        coupled = transposed(stacked[e], inverse[e]).astype(BF)
        product = transposed(coupled, back[e])
        schur_ref[e] = (diagonal[e].astype(F32).T - product[:width]).astype(BF)
        condensed = ends[row, :] - product[width : width + 1]
        condensed_ref[row, :] = condensed.astype(BF).astype(F32)

    if not early:

        @pl.when(wraps)
        def _():
            schur_ref[...] = done[first:]


def condense(first, count, dom_count, blocks, small, done=()):
    elements, inner, _ = blocks[0].shape
    width = blocks[3].shape[1]
    room = elements - first

    def kernel(*refs):
        condense_kernel(first, count, dom_count, *refs)

    out_shape = (
        jax.ShapeDtypeStruct((room, width, width), BF),
        jax.ShapeDtypeStruct((GROUP, width), F32),
    )
    shapes = ((room, inner, inner), (room, width + BLOCK, inner), (room, width, inner), (room, width, width))
    scratch = [pltpu.VMEM(shape, BF) for shape in shapes]
    scratch += [pltpu.VMEM((GROUP, inner), F32), pltpu.VMEM((GROUP, width), F32)]
    scratch += [pltpu.SemaphoreType.DMA((room, 4)), pltpu.SemaphoreType.DMA((len(small),))]
    scratch += [pltpu.VMEM(array.shape, array.dtype) for array in small]
    if first == 0:
        out_shape += route_shapes(dom_count)
        scratch += [pltpu.VMEM((GROUP, LANES), jnp.int32)] * 2
    flops = 2 * count * (inner * inner * width + inner * width * width)
    hbm = [pl.BlockSpec(memory_space=pltpu.HBM)] * (len(blocks) + len(small))
    return pl.pallas_call(
        kernel,
        in_specs=hbm + [pl.BlockSpec(memory_space=pltpu.VMEM)] * len(done),
        out_shape=out_shape,
        scratch_shapes=scratch,
        compiler_params=params(24),
        cost_estimate=pl.CostEstimate(flops=flops, bytes_accessed=count * 3_000_000, transcendentals=0),
        name="condense",
    )(*in_hbm(*blocks, *small), *done)


def products(vectors, early_ref, late_ref):
    terms = jnp.zeros(vectors.shape, F32)
    elements = early_ref.shape[0]
    early = elements - late_ref.shape[0]
    for e in range(elements):
        block = early_ref[e] if e < early else late_ref[e - early]
        part = jnp.dot(vectors, block, preferred_element_type=F32)
        terms = jnp.where(iota(terms.shape, 0) == e, part, terms)
    return terms


def gather_wide(values, wide, face_width):
    for k in range(SIDES):
        wide[:, k * face_width : (k + 1) * face_width] = values[k * GROUP : (k + 1) * GROUP, :face_width]
    return wide[...].astype(BF)


def split_rows(wide, tall, face_width):
    tall[...] = jnp.zeros(tall.shape, F32)
    for k in range(SIDES):
        tall[k * GROUP : (k + 1) * GROUP, :face_width] = wide[:, k * face_width : (k + 1) * face_width]
    return tall[...]


def first_kernel(
    face_width,
    here_ref,
    above_ref,
    schur_a,
    schur_b,
    condensed_a,
    condensed_b,
    pick_ref,
    compact_ref,
    own_ref,
    up_ref,
    down_ref,
    key_ref,
    own_out,
    up_out,
    down_out,
    terms_out,
    key_out,
    wide,
    tall,
):
    table = jnp.concatenate([here_ref[...], above_ref[...]], axis=0)
    values = jnp.dot(pick_ref[...], table, preferred_element_type=F32)
    face = 16.0 + jnp.broadcast_to(values[:, FACE_LANE : FACE_LANE + 1], values.shape)
    vectors = gather_wide(values, wide, face_width)
    wide[...] = products(vectors, schur_a, schur_b) - (condensed_a[...] + condensed_b[...])
    rows = split_rows(wide, tall, face_width)
    terms_out[...] = rows
    key_out[...] = face * key_ref[...]
    packed = jnp.dot(compact_ref[...], rows.astype(BF), preferred_element_type=F32)
    held = packed[:BLOCK]
    lifted = packed[BLOCK:]
    lane = iota((BLOCK, LANES), 1)
    line = iota((BLOCK, LANES), 0)

    def key_row(ref, index):
        return jnp.where(line == index, jnp.sum(face * ref[...], axis=0, keepdims=True), 0.0)

    def main(block, far):
        return pltpu.roll(jnp.where(lane < KEY_LANE, block, 0.0), KEY_LANE if far else 0, axis=1)

    def tail(block, index):
        ends = jnp.where((lane >= KEY_LANE) & (lane < face_width), block, 0.0)
        place = LANES - KEY_LANE + 2 * index * WIDE
        upper = pltpu.roll(ends[:GROUP], place % LANES, axis=1)
        return upper + pltpu.roll(ends[GROUP:], (place + WIDE) % LANES, axis=1)

    up_keys = key_row(up_ref, BLOCK - 1)
    own_out[:BLOCK] = (main(held, False) + key_row(own_ref, BLOCK - 1)).astype(BF)
    own_out[BLOCK : 2 * BLOCK] = (main(lifted, False) - pltpu.roll(up_keys, KEY_LANE, axis=1)).astype(BF)
    none = jnp.zeros((GROUP, LANES), F32)
    own_out[2 * BLOCK :] = jnp.concatenate([tail(held, 0) + tail(lifted, 1), none], axis=0).astype(BF)
    up_out[:BLOCK] = (main(lifted, True) + up_keys).astype(BF)
    up_out[BLOCK:] = jnp.concatenate([tail(lifted, 2), none], axis=0).astype(BF)
    down_out[:BLOCK] = (main(held, True) + key_row(down_ref, BLOCK - 1)).astype(BF)
    down_out[BLOCK:] = jnp.concatenate([tail(held, 3), none], axis=0).astype(BF)


def first_terms(face_width, *arrays):
    width = arrays[2].shape[1]

    def kernel(*refs):
        first_kernel(face_width, *refs)

    return pl.pallas_call(
        kernel,
        out_shape=(
            jax.ShapeDtypeStruct((3 * BLOCK, LANES), BF),
            jax.ShapeDtypeStruct((2 * BLOCK, LANES), BF),
            jax.ShapeDtypeStruct((2 * BLOCK, LANES), BF),
            jax.ShapeDtypeStruct((ROWS, LANES), F32),
            jax.ShapeDtypeStruct((ROWS, LANES), F32),
        ),
        scratch_shapes=[pltpu.VMEM((GROUP, width), F32), pltpu.VMEM((ROWS, LANES), F32)],
        compiler_params=params(),
        name="first_terms",
    )(*arrays)


def pack_kernel(own_ref, below_ref, above_ref, out_ref):
    own = own_ref[...].astype(F32)
    below = below_ref[...].astype(F32)
    above = above_ref[...].astype(F32)
    start = own[:BLOCK] + below[:BLOCK]
    middle = own[BLOCK : 2 * BLOCK] + above[:BLOCK]
    ends = own[2 * BLOCK :] + below[BLOCK:] + above[BLOCK:]
    rows = jnp.concatenate([start, middle, ends[:GROUP]], axis=0).astype(BF)
    for d in range(out_ref.shape[0]):
        out_ref[d] = rows


def pack(dom_count, own, below, above):
    return pl.pallas_call(
        pack_kernel,
        out_shape=jax.ShapeDtypeStruct((dom_count, PACKED, LANES), BF),
        compiler_params=params(4),
        name="pack",
    )(own, below, above)


def second_kernel(
    face_width, slab_ref, terms_ref, key_ref, schur_a, schur_b, put_ref, code_ref, held_out, lifted_out, wide, tall
):
    devices = slab_ref.shape[0]
    depth = devices * BLOCK
    chunks = depth // LANES
    start = slab_ref[:, :BLOCK, :].reshape(depth, LANES)
    middle = slab_ref[:, BLOCK : 2 * BLOCK, :].reshape(depth, LANES)
    ends = slab_ref[:, 2 * BLOCK :, :].astype(F32)
    ends = jnp.concatenate([ends, ends], axis=1).reshape(depth, LANES)
    upper = lax.rem(lax.div(iota((depth, LANES), 1), WIDE), 2) == lax.div(lax.rem(iota((depth, LANES), 0), BLOCK), GROUP)
    ends = jnp.where(upper, ends, 0.0).astype(BF)
    shape = (2 * GROUP, depth)
    half = lax.div(iota(shape, 0), GROUP)
    chunk = lax.rem(iota(shape, 0), GROUP)
    column = iota(shape, 1)
    chosen = (lax.rem(column, BLOCK) == BLOCK - 1) & (lax.div(column, LANES // 2) == 2 * chunk + half)
    chosen = jnp.where(chosen, 1.0, 0.0).astype(BF)
    lane = iota((GROUP, LANES), 1)
    key = key_ref[...]

    def block_keys(rows):
        found = jnp.dot(chosen, rows, preferred_element_type=F32)
        low, high = found[:GROUP], found[GROUP:]
        near = jnp.where(lane < KEY_LANE, low, pltpu.roll(high, KEY_LANE, axis=1))
        far = jnp.where(lane < KEY_LANE, pltpu.roll(low, KEY_LANE, axis=1), high)
        return near, far

    outer_keys = block_keys(start)
    inner_keys = block_keys(middle)
    keys = (outer_keys[0], inner_keys[0], outer_keys[1], inner_keys[1])

    def match(b):
        return jnp.concatenate(
            [jnp.where(key == keys[b][c : c + 1], 1.0, 0.0).astype(BF) for c in range(chunks)], axis=1
        )

    matches = [match(b) for b in range(4)]
    outer = jnp.dot(jnp.concatenate([matches[0], matches[2]], axis=0), start, preferred_element_type=F32)
    inner = jnp.dot(jnp.concatenate([matches[1], matches[3]], axis=0), middle, preferred_element_type=F32)
    last = jnp.dot(jnp.concatenate(matches, axis=0), ends, preferred_element_type=F32)
    lane = iota((ROWS, LANES), 1)
    near = outer[:ROWS] + inner[:ROWS]
    far = outer[ROWS:] + inner[ROWS:]
    both = jnp.where(lane < KEY_LANE, near + pltpu.roll(far, KEY_LANE, axis=1), 0.0)
    for b in range(4):
        line = last[b * ROWS : (b + 1) * ROWS]
        place = LANES + KEY_LANE - 2 * b * WIDE
        moved = pltpu.roll(line, place % LANES, axis=1) + pltpu.roll(line, (place - WIDE) % LANES, axis=1)
        both = both + jnp.where((lane >= KEY_LANE) & (lane < face_width), moved, 0.0)
    first = terms_ref[...]
    residual = both + (first - first.astype(BF).astype(F32))
    vectors = gather_wide(residual, wide, face_width)
    wide[...] = products(vectors, schur_a, schur_b)
    second = split_rows(wide, tall, face_width)
    pair = jnp.concatenate([first, second], axis=1)
    placed = exact_dot(put_ref[...], pair)
    positions = held_out.shape[0]
    held_out[...] = placed[:positions]
    codes = jnp.concatenate([code_ref[...], code_ref[...]], axis=1)[:1]
    lifted_out[...] = jnp.where(iota(lifted_out.shape, 0) == BLOCK - 1, codes, placed[positions:])


def second_terms(face_width, positions, *arrays):
    width = arrays[3].shape[1]

    def kernel(*refs):
        second_kernel(face_width, *refs)

    return pl.pallas_call(
        kernel,
        out_shape=(
            jax.ShapeDtypeStruct((positions, 2 * LANES), F32),
            jax.ShapeDtypeStruct((BLOCK, 2 * LANES), F32),
        ),
        scratch_shapes=[pltpu.VMEM((GROUP, width), F32), pltpu.VMEM((ROWS, LANES), F32)],
        compiler_params=params(),
        name="second_terms",
    )(*arrays)


def merge_kernel(held_ref, raised_ref, out_ref):
    raised = raised_ref[...]
    code = raised[BLOCK - 1 :, :BLOCK]
    place = iota((out_ref.shape[0], BLOCK), 0).astype(F32)
    onehot = jnp.where(place == code, 1.0, 0.0)
    out_ref[...] = held_ref[...] + exact_dot(onehot.astype(BF), raised)


def merge(held, raised):
    return pl.pallas_call(
        merge_kernel,
        out_shape=jax.ShapeDtypeStruct(held.shape, F32),
        compiler_params=params(4),
        name="merge",
    )(held, raised)


def collect_kernel(arrived_ref, slots_ref, residual_ref, image_ref, slots):
    faces, width = residual_ref.shape
    onehot = face_onehot(slots_ref, slots, arrived_ref.shape[0])
    onehot = jnp.concatenate([onehot, jnp.zeros((onehot.shape[0], LANES - BLOCK), F32)], axis=1)
    total = exact_dot(onehot.T[:BLOCK].astype(BF), arrived_ref[...])
    residual_ref[...] = total[:faces, :width]
    image_ref[...] = total[:faces, LANES : LANES + width]


def collect(arrived, slots, faces, width):
    out = jax.ShapeDtypeStruct((faces, width), F32)
    return pl.pallas_call(
        collect_kernel,
        out_shape=(out, out),
        scratch_shapes=[pltpu.VMEM((2, BLOCK), jnp.int32)],
        compiler_params=params(4),
        name="collect",
    )(arrived, slots)


def on_device(
    local_inverse,
    local_trace,
    trace_local,
    trace_trace,
    local_rhs,
    trace_rhs,
    trace_state,
    side_owner,
    side_slot,
    face_slots,
):
    dom_count = lax.axis_size("dom")
    faces, face_width = trace_state.shape
    positions = 2 * dom_count
    slots = face_slots.T
    blocks = (local_inverse, jnp.swapaxes(local_trace, 1, 2), trace_local, trace_trace)
    outgoing = spread(slots, trace_state, positions)
    here = exchange(outgoing.reshape(dom_count, 2, LANES)).reshape(positions, LANES)
    elements = local_inverse.shape[0]
    early = elements - max(elements // 5, 1)
    schur_a, condensed_a, pick, put, compact, codes, own_keys, up_keys, down_keys, keys = condense(
        0, early, dom_count, blocks, (local_rhs, trace_rhs, side_owner, side_slot)
    )
    here, schur_a, boundary = lax.optimization_barrier((here, schur_a, trace_rhs))
    above = shift(here, -1)
    schur_b, condensed_b = condense(
        early, elements - early, dom_count, blocks, (local_rhs, boundary), (schur_a,)
    )
    own, lifted, held, terms, key = first_terms(
        face_width,
        here,
        above,
        schur_a,
        schur_b,
        condensed_a,
        condensed_b,
        pick,
        compact,
        own_keys,
        up_keys,
        down_keys,
        keys,
    )
    slab = exchange(pack(dom_count, own, shift(lifted, 1), shift(held, -1)))
    stay, rise = second_terms(face_width, positions, slab, terms, key, schur_a, schur_b, put, codes)
    arriving = merge(stay, shift(rise, 1))
    arrived = exchange(arriving.reshape(dom_count, 2, 2 * LANES)).reshape(positions, 2 * LANES)
    return collect(arrived, slots, faces, face_width)


def solution(mesh):
    both = ("grp", "dom")
    blocks = (P(both, None, None),) * 4
    rows = (P(both, None),) * 6
    return jax.shard_map(
        on_device,
        mesh=mesh,
        in_specs=blocks + rows,
        out_specs=(P(both, None), P(both, None)),
        check_vma=False,
    )
```

```python
import jax
import jax.numpy as jnp
from jax import lax
from jax.experimental import pallas as pl
from jax.experimental.pallas import tpu as pltpu
from jax.sharding import PartitionSpec as P

BF = jnp.bfloat16
F32 = jnp.float32
LANES = 128
SIDES = 6
GROUP = 8
ROWS = SIDES * GROUP
BLOCK = 16
FACE_LANE = 80
KEY_LANE = 64
WIDE = 16
PACKED = 40


def iota(shape, dim):
    return lax.broadcasted_iota(jnp.int32, shape, dim)


def params(mib=12):
    return pltpu.CompilerParams(vmem_limit_bytes=mib * 1024 * 1024)


def in_hbm(*arrays):
    return [pltpu.with_memory_space_constraint(array, pltpu.HBM) for array in arrays]


def shift(payload, by):
    devices = lax.axis_size("grp")
    return lax.ppermute(payload, "grp", [(i, (i + by) % devices) for i in range(devices)])


def exchange(payload):
    return lax.all_to_all(payload, "dom", split_axis=0, concat_axis=0, tiled=True)


def face_onehot(slots_ref, scratch, positions):
    scratch[...] = jnp.full(scratch.shape, -1, jnp.int32)
    scratch[:, : slots_ref.shape[1]] = slots_ref[...]
    place = iota((positions, BLOCK), 0)
    hit = (place == scratch[0:1, :]) | (place == scratch[1:2, :])
    return jnp.where(hit, 1.0, 0.0)


def spread_kernel(slots_from, state_from, out_ref, slots_ref, state_ref, slots, rows, sems):
    copies = [
        pltpu.make_async_copy(slots_from, slots_ref, sems.at[0]),
        pltpu.make_async_copy(state_from, state_ref, sems.at[1]),
    ]
    for copy in copies:
        copy.start()
    for copy in copies:
        copy.wait()
    faces, width = state_ref.shape
    rows[...] = jnp.zeros(rows.shape, F32)
    rows[:faces, :width] = state_ref[...].astype(F32)
    lane = iota(rows.shape, 1)
    index = iota(rows.shape, 0).astype(F32)
    table = jnp.where(lane == FACE_LANE, index, rows[...]).astype(BF)
    onehot = face_onehot(slots_ref, slots, out_ref.shape[0]).astype(BF)
    out_ref[...] = jnp.dot(onehot, table, preferred_element_type=F32).astype(BF)


def spread(slots, state, positions):
    return pl.pallas_call(
        spread_kernel,
        in_specs=[pl.BlockSpec(memory_space=pltpu.HBM)] * 2,
        out_shape=jax.ShapeDtypeStruct((positions, LANES), BF),
        scratch_shapes=[
            pltpu.VMEM(slots.shape, slots.dtype),
            pltpu.VMEM(state.shape, state.dtype),
            pltpu.VMEM((2, BLOCK), jnp.int32),
            pltpu.VMEM((BLOCK, LANES), F32),
            pltpu.SemaphoreType.DMA((2,)),
        ],
        compiler_params=params(4),
        name="spread",
    )(*in_hbm(slots, state))


def fill_routes(
    dom_count, owner_ref, slot_ref, pick_ref, put_ref, compact_ref, code_ref, own_ref, up_ref, down_ref, key_ref, owners, slots
):
    elements = owner_ref.shape[0]
    owners[...] = jnp.full(owners.shape, -1, jnp.int32)
    slots[...] = jnp.zeros(slots.shape, jnp.int32)
    owners[:elements, :SIDES] = owner_ref[...]
    slots[:elements, :SIDES] = slot_ref[...]

    def rows(ref):
        return jnp.concatenate([jnp.broadcast_to(ref[:, k : k + 1], (GROUP, LANES)) for k in range(SIDES)], axis=0)

    owner = rows(owners)
    slot = rows(slots)
    grp = lax.axis_index("grp")
    part = lax.axis_index("dom") % 4
    valid = owner >= 0
    owner = jnp.maximum(owner, 0)
    owner_dom = lax.rem(owner, dom_count)
    owner_grp = lax.div(owner, dom_count)
    lifted = valid & (owner_grp != grp)
    held = valid & (owner_grp == grp)
    lane = iota((ROWS, LANES), 1)
    place = owner_dom * 2 + slot
    pick = jnp.where(valid & (lane == place + jnp.where(lifted, 2 * dom_count, 0)), 1.0, 0.0)
    pick_ref[...] = pick.astype(BF)
    pad = jnp.zeros((LANES - ROWS, LANES), F32)
    filler = jnp.zeros((2 * LANES - 3 * ROWS, LANES), F32)

    def repeated(table):
        return jnp.concatenate([table, table, table, filler], axis=0).T[:, : 3 * ROWS].astype(BF)

    put_ref[: 2 * dom_count] = repeated(pick)[: 2 * dom_count]
    before = jnp.where(iota((ROWS, ROWS), 1) < iota((ROWS, ROWS), 0), 1.0, 0.0).astype(BF)

    def rank(flag):
        counts = jnp.dot(before, jnp.where(flag, 1.0, 0.0).astype(BF), preferred_element_type=F32)
        return counts.astype(jnp.int32)

    order = jnp.where(lifted, rank(lifted), rank(held))
    seat = valid & (lane == order + jnp.where(lifted, BLOCK, 0))
    seats = jnp.where(seat, 1.0, 0.0)
    compact = jnp.concatenate([seats, pad], axis=0).T
    compact_ref[...] = compact[: 2 * BLOCK, :ROWS].astype(BF)
    put_ref[2 * dom_count :] = repeated(seats)[BLOCK : 2 * BLOCK]
    code = jnp.where(lifted & ((lane & (BLOCK - 1)) == order), place.astype(F32) + 1.0, 0.0)
    code_ref[...] = jnp.broadcast_to(jnp.sum(code, axis=0, keepdims=True) - 1.0, code_ref.shape)
    power = jnp.full((ROWS, LANES), 2.0**-16, F32)
    for bit in range(5):
        power = power * jnp.where((owner_dom & (1 << bit)) != 0, 2.0 ** (1 << bit), 1.0)
    signed = jnp.where(lifted, -power, power)
    key_lane = lane == order + KEY_LANE + part * BLOCK
    own_ref[...] = jnp.where(held & (lane == order + part * BLOCK), signed, 0.0)
    up_ref[...] = jnp.where(lifted & key_lane, power, 0.0)
    down_ref[...] = jnp.where(held & key_lane, -power, 0.0)
    key_ref[...] = jnp.where(valid, signed, 2.0**-40)


def route_shapes(dom_count):
    def table(rows, columns, dtype):
        return jax.ShapeDtypeStruct((rows, columns), dtype)

    full = table(ROWS, LANES, F32)
    return (
        table(ROWS, LANES, BF),
        table(2 * dom_count + BLOCK, 3 * ROWS, BF),
        table(2 * BLOCK, ROWS, BF),
        table(GROUP, LANES, F32),
        full,
        full,
        full,
        full,
    )


def exact_dot(onehot, values):
    high = values.astype(BF)
    rest = values - high.astype(F32)
    middle = rest.astype(BF)
    low = (rest - middle.astype(F32)).astype(BF)
    return jnp.dot(onehot, jnp.concatenate([high, middle, low], axis=0), preferred_element_type=F32)


def transposed(left, right):
    return lax.dot_general(left, right, (((1,), (1,)), ((), ())), preferred_element_type=F32)


def condense_kernel(first, count, dom_count, *refs):
    early = first == 0
    sources, refs = refs[:4], refs[4:]
    small, refs = (refs[:4], refs[4:]) if early else (refs[:2], refs[2:])
    done, refs = (None, refs) if early else (refs[0], refs[1:])
    schur_ref, condensed_ref = refs[:2]
    tables = refs[2:10] if early else ()
    inverse, stacked, back, diagonal, rows, ends, sems, small_sems, *arrived = refs[2 + len(tables) :]
    routing = arrived[len(small) :]
    arrived = arrived[: len(small)]
    width = diagonal.shape[1]
    elements = small[0].shape[0]
    wraps = lax.axis_index("grp") == 0
    last = jnp.where(wraps, elements, count) if early else jnp.where(wraps, 0, count)
    small_copies = [
        pltpu.make_async_copy(source, target, small_sems.at[i]) for i, (source, target) in enumerate(zip(small, arrived))
    ]

    def copies(e):
        targets = (inverse.at[e], stacked.at[e, pl.ds(0, width)], back.at[e], diagonal.at[e])
        return [
            pltpu.make_async_copy(source.at[first + e], target, sems.at[e, i])
            for i, (source, target) in enumerate(zip(sources, targets))
        ]

    for copy in small_copies:
        copy.start()

    @pl.loop(0, last)
    def _(e):
        for copy in copies(e):
            copy.start()

    for copy in small_copies:
        copy.wait()
    if early:
        fill_routes(dom_count, arrived[2], arrived[3], *tables, *routing)
    condensed_ref[...] = jnp.zeros(condensed_ref.shape, F32)
    rows[:elements] = arrived[0][...].astype(F32)
    ends[:elements] = arrived[1][...].astype(F32)

    @pl.loop(0, last)
    def _(e):
        row = pl.ds(first + e, 1)
        right = jnp.broadcast_to(rows[row, :], (BLOCK, rows.shape[1]))
        stacked[e, width:] = right.astype(BF)
        for copy in copies(e):
            copy.wait()
        coupled = transposed(stacked[e], inverse[e]).astype(BF)
        product = transposed(coupled, back[e])
        schur_ref[e] = (diagonal[e].astype(F32).T - product[:width]).astype(BF)
        condensed = ends[row, :] - product[width : width + 1]
        condensed_ref[row, :] = condensed.astype(BF).astype(F32)

    if not early:

        @pl.when(wraps)
        def _():
            schur_ref[...] = done[first:]


def condense(first, count, dom_count, blocks, small, done=()):
    elements, inner, _ = blocks[0].shape
    width = blocks[3].shape[1]
    room = elements - first

    def kernel(*refs):
        condense_kernel(first, count, dom_count, *refs)

    out_shape = (
        jax.ShapeDtypeStruct((room, width, width), BF),
        jax.ShapeDtypeStruct((GROUP, width), F32),
    )
    shapes = ((room, inner, inner), (room, width + BLOCK, inner), (room, width, inner), (room, width, width))
    scratch = [pltpu.VMEM(shape, BF) for shape in shapes]
    scratch += [pltpu.VMEM((GROUP, inner), F32), pltpu.VMEM((GROUP, width), F32)]
    scratch += [pltpu.SemaphoreType.DMA((room, 4)), pltpu.SemaphoreType.DMA((len(small),))]
    scratch += [pltpu.VMEM(array.shape, array.dtype) for array in small]
    if first == 0:
        out_shape += route_shapes(dom_count)
        scratch += [pltpu.VMEM((GROUP, LANES), jnp.int32)] * 2
    flops = 2 * count * (inner * inner * width + inner * width * width)
    hbm = [pl.BlockSpec(memory_space=pltpu.HBM)] * (len(blocks) + len(small))
    return pl.pallas_call(
        kernel,
        in_specs=hbm + [pl.BlockSpec(memory_space=pltpu.VMEM)] * len(done),
        out_shape=out_shape,
        scratch_shapes=scratch,
        compiler_params=params(24),
        cost_estimate=pl.CostEstimate(flops=flops, bytes_accessed=count * 3_000_000, transcendentals=0),
        name="condense",
    )(*in_hbm(*blocks, *small), *done)


def products(vectors, early_ref, late_ref):
    terms = jnp.zeros(vectors.shape, F32)
    elements = early_ref.shape[0]
    early = elements - late_ref.shape[0]
    for e in range(elements):
        block = early_ref[e] if e < early else late_ref[e - early]
        part = jnp.dot(vectors, block, preferred_element_type=F32)
        terms = jnp.where(iota(terms.shape, 0) == e, part, terms)
    return terms


def gather_wide(values, wide, face_width):
    for k in range(SIDES):
        wide[:, k * face_width : (k + 1) * face_width] = values[k * GROUP : (k + 1) * GROUP, :face_width]
    return wide[...].astype(BF)


def split_rows(wide, tall, face_width):
    tall[...] = jnp.zeros(tall.shape, F32)
    for k in range(SIDES):
        tall[k * GROUP : (k + 1) * GROUP, :face_width] = wide[:, k * face_width : (k + 1) * face_width]
    return tall[...]


def first_kernel(
    face_width,
    here_ref,
    above_ref,
    schur_a,
    schur_b,
    condensed_a,
    condensed_b,
    pick_ref,
    compact_ref,
    own_ref,
    up_ref,
    down_ref,
    key_ref,
    own_out,
    up_out,
    down_out,
    terms_out,
    key_out,
    wide,
    tall,
):
    table = jnp.concatenate([here_ref[...], above_ref[...]], axis=0)
    values = jnp.dot(pick_ref[...], table, preferred_element_type=F32)
    face = 16.0 + jnp.broadcast_to(values[:, FACE_LANE : FACE_LANE + 1], values.shape)
    vectors = gather_wide(values, wide, face_width)
    wide[...] = products(vectors, schur_a, schur_b) - (condensed_a[...] + condensed_b[...])
    rows = split_rows(wide, tall, face_width)
    terms_out[...] = rows
    key_out[...] = face * key_ref[...]
    packed = jnp.dot(compact_ref[...], rows.astype(BF), preferred_element_type=F32)
    held = packed[:BLOCK]
    lifted = packed[BLOCK:]
    lane = iota((BLOCK, LANES), 1)
    line = iota((BLOCK, LANES), 0)

    def key_row(ref, index):
        return jnp.where(line == index, jnp.sum(face * ref[...], axis=0, keepdims=True), 0.0)

    def main(block, far):
        return pltpu.roll(jnp.where(lane < KEY_LANE, block, 0.0), KEY_LANE if far else 0, axis=1)

    def tail(block, index):
        ends = jnp.where((lane >= KEY_LANE) & (lane < face_width), block, 0.0)
        place = LANES - KEY_LANE + 2 * index * WIDE
        upper = pltpu.roll(ends[:GROUP], place % LANES, axis=1)
        return upper + pltpu.roll(ends[GROUP:], (place + WIDE) % LANES, axis=1)

    up_keys = key_row(up_ref, BLOCK - 1)
    own_out[:BLOCK] = (main(held, False) + key_row(own_ref, BLOCK - 1)).astype(BF)
    own_out[BLOCK : 2 * BLOCK] = (main(lifted, False) - pltpu.roll(up_keys, KEY_LANE, axis=1)).astype(BF)
    none = jnp.zeros((GROUP, LANES), F32)
    own_out[2 * BLOCK :] = jnp.concatenate([tail(held, 0) + tail(lifted, 1), none], axis=0).astype(BF)
    up_out[:BLOCK] = (main(lifted, True) + up_keys).astype(BF)
    up_out[BLOCK:] = jnp.concatenate([tail(lifted, 2), none], axis=0).astype(BF)
    down_out[:BLOCK] = (main(held, True) + key_row(down_ref, BLOCK - 1)).astype(BF)
    down_out[BLOCK:] = jnp.concatenate([tail(held, 3), none], axis=0).astype(BF)


def first_terms(face_width, *arrays):
    width = arrays[2].shape[1]

    def kernel(*refs):
        first_kernel(face_width, *refs)

    return pl.pallas_call(
        kernel,
        out_shape=(
            jax.ShapeDtypeStruct((3 * BLOCK, LANES), BF),
            jax.ShapeDtypeStruct((2 * BLOCK, LANES), BF),
            jax.ShapeDtypeStruct((2 * BLOCK, LANES), BF),
            jax.ShapeDtypeStruct((ROWS, LANES), F32),
            jax.ShapeDtypeStruct((ROWS, LANES), F32),
        ),
        scratch_shapes=[pltpu.VMEM((GROUP, width), F32), pltpu.VMEM((ROWS, LANES), F32)],
        compiler_params=params(),
        name="first_terms",
    )(*arrays)


def pack_kernel(own_ref, below_ref, above_ref, out_ref):
    own = own_ref[...].astype(F32)
    below = below_ref[...].astype(F32)
    above = above_ref[...].astype(F32)
    start = own[:BLOCK] + below[:BLOCK]
    middle = own[BLOCK : 2 * BLOCK] + above[:BLOCK]
    ends = own[2 * BLOCK :] + below[BLOCK:] + above[BLOCK:]
    rows = jnp.concatenate([start, middle, ends[:GROUP]], axis=0).astype(BF)
    for d in range(out_ref.shape[0]):
        out_ref[d] = rows


def pack(dom_count, own, below, above):
    return pl.pallas_call(
        pack_kernel,
        out_shape=jax.ShapeDtypeStruct((dom_count, PACKED, LANES), BF),
        compiler_params=params(4),
        name="pack",
    )(own, below, above)


def second_kernel(
    face_width, slab_ref, terms_ref, key_ref, schur_a, schur_b, put_ref, code_ref, held_out, lifted_out, wide, tall
):
    devices = slab_ref.shape[0]
    depth = devices * BLOCK
    chunks = depth // LANES
    start = slab_ref[:, :BLOCK, :].reshape(depth, LANES)
    middle = slab_ref[:, BLOCK : 2 * BLOCK, :].reshape(depth, LANES)
    ends = slab_ref[:, 2 * BLOCK :, :].astype(F32)
    ends = jnp.concatenate([ends, ends], axis=1).reshape(depth, LANES)
    wanted = ((iota((depth, LANES), 1) & WIDE) != 0) == ((iota((depth, LANES), 0) & GROUP) != 0)
    ends = jnp.where(wanted, ends, 0.0).astype(BF)
    shape = (2 * GROUP, depth)
    line = iota(shape, 0)
    column = iota(shape, 1)
    group = 2 * (line & (GROUP - 1)) + (line >> 3)
    chosen = ((column & (BLOCK - 1)) == BLOCK - 1) & ((column >> 6) == group)
    chosen = jnp.where(chosen, 1.0, 0.0).astype(BF)
    lane = iota((GROUP, LANES), 1)
    key = key_ref[...]

    def block_keys(rows):
        found = jnp.dot(chosen, rows, preferred_element_type=F32)
        low, high = found[:GROUP], found[GROUP:]
        near = jnp.where(lane < KEY_LANE, low, pltpu.roll(high, KEY_LANE, axis=1))
        far = jnp.where(lane < KEY_LANE, pltpu.roll(low, KEY_LANE, axis=1), high)
        return near, far

    outer_keys = block_keys(start)
    inner_keys = block_keys(middle)
    keys = (outer_keys[0], inner_keys[0], outer_keys[1], inner_keys[1])

    def match(b):
        return jnp.concatenate(
            [jnp.where(key == keys[b][c : c + 1], 1.0, 0.0).astype(BF) for c in range(chunks)], axis=1
        )

    matches = [match(b) for b in range(4)]
    outer = jnp.dot(jnp.concatenate([matches[0], matches[2]], axis=0), start, preferred_element_type=F32)
    inner = jnp.dot(jnp.concatenate([matches[1], matches[3]], axis=0), middle, preferred_element_type=F32)
    last = jnp.dot(jnp.concatenate(matches, axis=0), ends, preferred_element_type=F32)
    lane = iota((ROWS, LANES), 1)
    near = outer[:ROWS] + inner[:ROWS]
    far = outer[ROWS:] + inner[ROWS:]
    both = jnp.where(lane < KEY_LANE, near + pltpu.roll(far, KEY_LANE, axis=1), 0.0)
    for b in range(4):
        line = last[b * ROWS : (b + 1) * ROWS]
        place = LANES + KEY_LANE - 2 * b * WIDE
        moved = pltpu.roll(line, place % LANES, axis=1) + pltpu.roll(line, (place - WIDE) % LANES, axis=1)
        both = both + jnp.where((lane >= KEY_LANE) & (lane < face_width), moved, 0.0)
    first = terms_ref[...]
    residual = both + (first - first.astype(BF).astype(F32))
    vectors = gather_wide(residual, wide, face_width)
    wide[...] = products(vectors, schur_a, schur_b)
    second = split_rows(wide, tall, face_width)
    pair = jnp.concatenate([first, second], axis=1)
    placed = exact_dot(put_ref[...], pair)
    positions = held_out.shape[0]
    held_out[...] = placed[:positions]
    codes = jnp.concatenate([code_ref[...], code_ref[...]], axis=1)[:1]
    lifted_out[...] = jnp.where(iota(lifted_out.shape, 0) == BLOCK - 1, codes, placed[positions:])


def second_terms(face_width, positions, *arrays):
    width = arrays[3].shape[1]

    def kernel(*refs):
        second_kernel(face_width, *refs)

    return pl.pallas_call(
        kernel,
        out_shape=(
            jax.ShapeDtypeStruct((positions, 2 * LANES), F32),
            jax.ShapeDtypeStruct((BLOCK, 2 * LANES), F32),
        ),
        scratch_shapes=[pltpu.VMEM((GROUP, width), F32), pltpu.VMEM((ROWS, LANES), F32)],
        compiler_params=params(),
        name="second_terms",
    )(*arrays)


def merge_kernel(held_ref, raised_ref, out_ref):
    raised = raised_ref[...]
    code = raised[BLOCK - 1 :, : 3 * BLOCK]
    place = iota((out_ref.shape[0], 3 * BLOCK), 0).astype(F32)
    onehot = jnp.where(place == code, 1.0, 0.0)
    out_ref[...] = held_ref[...] + exact_dot(onehot.astype(BF), raised)


def merge(held, raised):
    return pl.pallas_call(
        merge_kernel,
        out_shape=jax.ShapeDtypeStruct(held.shape, F32),
        compiler_params=params(4),
        name="merge",
    )(held, raised)


def collect_kernel(arrived_ref, slots_ref, residual_ref, image_ref, slots):
    faces, width = residual_ref.shape
    onehot = face_onehot(slots_ref, slots, arrived_ref.shape[0])
    positions = onehot.shape[0]
    onehot = jnp.concatenate([onehot, jnp.zeros((positions, LANES - BLOCK), F32)], axis=1)
    onehot = jnp.concatenate([onehot] * 4, axis=0).T[:BLOCK, : 3 * positions].astype(BF)
    total = exact_dot(onehot, arrived_ref[...])
    residual_ref[...] = total[:faces, :width]
    image_ref[...] = total[:faces, LANES : LANES + width]


def collect(arrived, slots, faces, width):
    out = jax.ShapeDtypeStruct((faces, width), F32)
    return pl.pallas_call(
        collect_kernel,
        out_shape=(out, out),
        scratch_shapes=[pltpu.VMEM((2, BLOCK), jnp.int32)],
        compiler_params=params(4),
        name="collect",
    )(arrived, slots)


def on_device(
    local_inverse,
    local_trace,
    trace_local,
    trace_trace,
    local_rhs,
    trace_rhs,
    trace_state,
    side_owner,
    side_slot,
    face_slots,
):
    dom_count = lax.axis_size("dom")
    faces, face_width = trace_state.shape
    positions = 2 * dom_count
    slots = face_slots.T
    blocks = (local_inverse, jnp.swapaxes(local_trace, 1, 2), trace_local, trace_trace)
    outgoing = spread(slots, trace_state, positions)
    here = exchange(outgoing.reshape(dom_count, 2, LANES)).reshape(positions, LANES)
    elements = local_inverse.shape[0]
    early = elements - max(elements // 5, 1)
    schur_a, condensed_a, pick, put, compact, codes, own_keys, up_keys, down_keys, keys = condense(
        0, early, dom_count, blocks, (local_rhs, trace_rhs, side_owner, side_slot)
    )
    here, schur_a, boundary = lax.optimization_barrier((here, schur_a, trace_rhs))
    above = shift(here, -1)
    schur_b, condensed_b = condense(
        early, elements - early, dom_count, blocks, (local_rhs, boundary), (schur_a,)
    )
    own, lifted, held, terms, key = first_terms(
        face_width,
        here,
        above,
        schur_a,
        schur_b,
        condensed_a,
        condensed_b,
        pick,
        compact,
        own_keys,
        up_keys,
        down_keys,
        keys,
    )
    slab = exchange(pack(dom_count, own, shift(lifted, 1), shift(held, -1)))
    stay, rise = second_terms(face_width, positions, slab, terms, key, schur_a, schur_b, put, codes)
    arriving = merge(stay, shift(rise, 1))
    arrived = exchange(arriving.reshape(dom_count, 2, 2 * LANES)).reshape(positions, 2 * LANES)
    return collect(arrived, slots, faces, face_width)


def solution(mesh):
    both = ("grp", "dom")
    blocks = (P(both, None, None),) * 4
    rows = (P(both, None),) * 6
    return jax.shard_map(
        on_device,
        mesh=mesh,
        in_specs=blocks + rows,
        out_specs=(P(both, None), P(both, None)),
        check_vma=False,
    )
```

```python
import jax
import jax.numpy as jnp
from jax import lax
from jax.experimental import pallas as pl
from jax.experimental.pallas import tpu as pltpu
from jax.sharding import PartitionSpec as P

BF = jnp.bfloat16
F32 = jnp.float32
LANES = 128
SIDES = 6
GROUP = 8
ROWS = SIDES * GROUP
BLOCK = 16
FACE_LANE = 80
KEY_LANE = 64
WIDE = 16
PACKED = 40


def iota(shape, dim):
    return lax.broadcasted_iota(jnp.int32, shape, dim)


def params(mib=12):
    return pltpu.CompilerParams(vmem_limit_bytes=mib * 1024 * 1024)


def in_hbm(*arrays):
    return [pltpu.with_memory_space_constraint(array, pltpu.HBM) for array in arrays]


def shift(payload, by):
    devices = lax.axis_size("grp")
    return lax.ppermute(payload, "grp", [(i, (i + by) % devices) for i in range(devices)])


def exchange(payload):
    return lax.all_to_all(payload, "dom", split_axis=0, concat_axis=0, tiled=True)


def face_onehot(slots_ref, scratch, positions):
    scratch[...] = jnp.full(scratch.shape, -1, jnp.int32)
    scratch[:, : slots_ref.shape[1]] = slots_ref[...]
    place = iota((positions, BLOCK), 0)
    hit = (place == scratch[0:1, :]) | (place == scratch[1:2, :])
    return jnp.where(hit, 1.0, 0.0)


def spread_kernel(slots_from, state_from, out_ref, slots_ref, state_ref, slots, rows, sems):
    copies = [
        pltpu.make_async_copy(slots_from, slots_ref, sems.at[0]),
        pltpu.make_async_copy(state_from, state_ref, sems.at[1]),
    ]
    for copy in copies:
        copy.start()
    for copy in copies:
        copy.wait()
    faces, width = state_ref.shape
    rows[...] = jnp.zeros(rows.shape, F32)
    rows[:faces, :width] = state_ref[...].astype(F32)
    lane = iota(rows.shape, 1)
    index = iota(rows.shape, 0).astype(F32)
    table = jnp.where(lane == FACE_LANE, index, rows[...]).astype(BF)
    onehot = face_onehot(slots_ref, slots, out_ref.shape[0]).astype(BF)
    out_ref[...] = jnp.dot(onehot, table, preferred_element_type=F32).astype(BF)


def spread(slots, state, positions):
    return pl.pallas_call(
        spread_kernel,
        in_specs=[pl.BlockSpec(memory_space=pltpu.HBM)] * 2,
        out_shape=jax.ShapeDtypeStruct((positions, LANES), BF),
        scratch_shapes=[
            pltpu.VMEM(slots.shape, slots.dtype),
            pltpu.VMEM(state.shape, state.dtype),
            pltpu.VMEM((2, BLOCK), jnp.int32),
            pltpu.VMEM((BLOCK, LANES), F32),
            pltpu.SemaphoreType.DMA((2,)),
        ],
        compiler_params=params(4),
        name="spread",
    )(*in_hbm(slots, state))


def fill_routes(
    dom_count, owner_ref, slot_ref, pick_ref, put_ref, compact_ref, code_ref, own_ref, up_ref, down_ref, key_ref, owners, slots
):
    elements = owner_ref.shape[0]
    owners[...] = jnp.full(owners.shape, -1, jnp.int32)
    slots[...] = jnp.zeros(slots.shape, jnp.int32)
    owners[:elements, :SIDES] = owner_ref[...]
    slots[:elements, :SIDES] = slot_ref[...]

    def rows(ref):
        return jnp.concatenate([jnp.broadcast_to(ref[:, k : k + 1], (GROUP, LANES)) for k in range(SIDES)], axis=0)

    owner = rows(owners)
    slot = rows(slots)
    grp = lax.axis_index("grp")
    part = lax.axis_index("dom") % 4
    valid = owner >= 0
    owner = jnp.maximum(owner, 0)
    owner_dom = lax.rem(owner, dom_count)
    owner_grp = lax.div(owner, dom_count)
    lifted = valid & (owner_grp != grp)
    held = valid & (owner_grp == grp)
    lane = iota((ROWS, LANES), 1)
    place = owner_dom * 2 + slot
    pick = jnp.where(valid & (lane == place + jnp.where(lifted, 2 * dom_count, 0)), 1.0, 0.0)
    pick_ref[...] = pick.astype(BF)
    pad = jnp.zeros((LANES - ROWS, LANES), F32)
    filler = jnp.zeros((2 * LANES - 3 * ROWS, LANES), F32)

    def repeated(table):
        return jnp.concatenate([table, table, table, filler], axis=0).T[:, : 3 * ROWS].astype(BF)

    put_ref[: 2 * dom_count] = repeated(pick)[: 2 * dom_count]
    before = jnp.where(iota((ROWS, ROWS), 1) < iota((ROWS, ROWS), 0), 1.0, 0.0).astype(BF)

    def rank(flag):
        counts = jnp.dot(before, jnp.where(flag, 1.0, 0.0).astype(BF), preferred_element_type=F32)
        return counts.astype(jnp.int32)

    order = jnp.where(lifted, rank(lifted), rank(held))
    seat = valid & (lane == order + jnp.where(lifted, BLOCK, 0))
    seats = jnp.where(seat, 1.0, 0.0)
    compact = jnp.concatenate([seats, pad], axis=0).T
    compact_ref[...] = compact[: 2 * BLOCK, :ROWS].astype(BF)
    put_ref[2 * dom_count :] = repeated(seats)[BLOCK : 2 * BLOCK]
    code = jnp.where(lifted & ((lane & (BLOCK - 1)) == order), place.astype(F32) + 1.0, 0.0)
    code_ref[...] = jnp.broadcast_to(jnp.sum(code, axis=0, keepdims=True) - 1.0, code_ref.shape)
    power = jnp.full((ROWS, LANES), 2.0**-16, F32)
    for bit in range(5):
        power = power * jnp.where((owner_dom & (1 << bit)) != 0, 2.0 ** (1 << bit), 1.0)
    signed = jnp.where(lifted, -power, power)
    key_lane = lane == order + KEY_LANE + part * BLOCK
    own_ref[...] = jnp.where(held & (lane == order + part * BLOCK), signed, 0.0)
    up_ref[...] = jnp.where(lifted & key_lane, power, 0.0)
    down_ref[...] = jnp.where(held & key_lane, -power, 0.0)
    key_ref[...] = jnp.where(valid, signed, 2.0**-40)


def route_shapes(dom_count):
    def table(rows, columns, dtype):
        return jax.ShapeDtypeStruct((rows, columns), dtype)

    full = table(ROWS, LANES, F32)
    return (
        table(ROWS, LANES, BF),
        table(2 * dom_count + BLOCK, 3 * ROWS, BF),
        table(2 * BLOCK, ROWS, BF),
        table(GROUP, LANES, F32),
        full,
        full,
        full,
        full,
    )


def exact_dot(onehot, values):
    high = values.astype(BF)
    rest = values - high.astype(F32)
    middle = rest.astype(BF)
    low = (rest - middle.astype(F32)).astype(BF)
    return jnp.dot(onehot, jnp.concatenate([high, middle, low], axis=0), preferred_element_type=F32)


def transposed(left, right):
    return lax.dot_general(left, right, (((1,), (1,)), ((), ())), preferred_element_type=F32)


def condense_kernel(first, count, dom_count, *refs):
    early = first == 0
    sources, refs = refs[:4], refs[4:]
    small, refs = (refs[:4], refs[4:]) if early else (refs[:2], refs[2:])
    done, refs = (None, refs) if early else (refs[0], refs[1:])
    schur_ref, condensed_ref = refs[:2]
    tables = refs[2:10] if early else ()
    inverse, stacked, back, diagonal, rows, ends, sems, small_sems, *arrived = refs[2 + len(tables) :]
    routing = arrived[len(small) :]
    arrived = arrived[: len(small)]
    width = diagonal.shape[1]
    elements = small[0].shape[0]
    wraps = lax.axis_index("grp") == 0
    last = jnp.where(wraps, elements, count) if early else jnp.where(wraps, 0, count)
    small_copies = [
        pltpu.make_async_copy(source, target, small_sems.at[i]) for i, (source, target) in enumerate(zip(small, arrived))
    ]

    def copies(e):
        targets = (inverse.at[e], stacked.at[e, pl.ds(0, width)], back.at[e], diagonal.at[e])
        return [
            pltpu.make_async_copy(source.at[first + e], target, sems.at[e, i])
            for i, (source, target) in enumerate(zip(sources, targets))
        ]

    for copy in small_copies:
        copy.start()

    @pl.loop(0, last)
    def _(e):
        for copy in copies(e):
            copy.start()

    for copy in small_copies:
        copy.wait()
    if early:
        fill_routes(dom_count, arrived[2], arrived[3], *tables, *routing)
    condensed_ref[...] = jnp.zeros(condensed_ref.shape, F32)
    rows[:elements] = arrived[0][...].astype(F32)
    ends[:elements] = arrived[1][...].astype(F32)

    def work(e):
        row = pl.ds(first + e, 1)
        right = jnp.broadcast_to(rows[row, :], (BLOCK, rows.shape[1]))
        stacked[e, width:] = right.astype(BF)
        for copy in copies(e):
            copy.wait()
        coupled = transposed(stacked[e], inverse[e]).astype(BF)
        product = transposed(coupled, back[e])
        schur_ref[e] = (diagonal[e].astype(F32).T - product[:width]).astype(BF)
        condensed = ends[row, :] - product[width : width + 1]
        condensed_ref[row, :] = condensed.astype(BF).astype(F32)

    if early:
        pl.loop(0, last)(work)
    else:

        @pl.when(jnp.logical_not(wraps))
        def _():
            for e in range(count):
                work(e)

        @pl.when(wraps)
        def _():
            schur_ref[...] = done[first:]


def condense(first, count, dom_count, blocks, small, done=()):
    elements, inner, _ = blocks[0].shape
    width = blocks[3].shape[1]
    room = elements - first

    def kernel(*refs):
        condense_kernel(first, count, dom_count, *refs)

    out_shape = (
        jax.ShapeDtypeStruct((room, width, width), BF),
        jax.ShapeDtypeStruct((GROUP, width), F32),
    )
    shapes = ((room, inner, inner), (room, width + BLOCK, inner), (room, width, inner), (room, width, width))
    scratch = [pltpu.VMEM(shape, BF) for shape in shapes]
    scratch += [pltpu.VMEM((GROUP, inner), F32), pltpu.VMEM((GROUP, width), F32)]
    scratch += [pltpu.SemaphoreType.DMA((room, 4)), pltpu.SemaphoreType.DMA((len(small),))]
    scratch += [pltpu.VMEM(array.shape, array.dtype) for array in small]
    if first == 0:
        out_shape += route_shapes(dom_count)
        scratch += [pltpu.VMEM((GROUP, LANES), jnp.int32)] * 2
    flops = 2 * count * (inner * inner * width + inner * width * width)
    hbm = [pl.BlockSpec(memory_space=pltpu.HBM)] * (len(blocks) + len(small))
    return pl.pallas_call(
        kernel,
        in_specs=hbm + [pl.BlockSpec(memory_space=pltpu.VMEM)] * len(done),
        out_shape=out_shape,
        scratch_shapes=scratch,
        compiler_params=params(24),
        cost_estimate=pl.CostEstimate(flops=flops, bytes_accessed=count * 3_000_000, transcendentals=0),
        name="condense",
    )(*in_hbm(*blocks, *small), *done)


def products(vectors, early_ref, late_ref):
    terms = jnp.zeros(vectors.shape, F32)
    elements = early_ref.shape[0]
    early = elements - late_ref.shape[0]
    for e in range(elements):
        block = early_ref[e] if e < early else late_ref[e - early]
        part = jnp.dot(vectors, block, preferred_element_type=F32)
        terms = jnp.where(iota(terms.shape, 0) == e, part, terms)
    return terms


def gather_wide(values, wide, face_width):
    for k in range(SIDES):
        wide[:, k * face_width : (k + 1) * face_width] = values[k * GROUP : (k + 1) * GROUP, :face_width]
    return wide[...].astype(BF)


def split_rows(wide, tall, face_width):
    tall[...] = jnp.zeros(tall.shape, F32)
    for k in range(SIDES):
        tall[k * GROUP : (k + 1) * GROUP, :face_width] = wide[:, k * face_width : (k + 1) * face_width]
    return tall[...]


def first_kernel(
    face_width,
    here_ref,
    above_ref,
    schur_a,
    schur_b,
    condensed_a,
    condensed_b,
    pick_ref,
    compact_ref,
    own_ref,
    up_ref,
    down_ref,
    key_ref,
    own_out,
    up_out,
    down_out,
    terms_out,
    key_out,
    wide,
    tall,
):
    table = jnp.concatenate([here_ref[...], above_ref[...]], axis=0)
    values = jnp.dot(pick_ref[...], table, preferred_element_type=F32)
    face = 16.0 + jnp.broadcast_to(values[:, FACE_LANE : FACE_LANE + 1], values.shape)
    vectors = gather_wide(values, wide, face_width)
    wide[...] = products(vectors, schur_a, schur_b) - (condensed_a[...] + condensed_b[...])
    rows = split_rows(wide, tall, face_width)
    terms_out[...] = rows
    key_out[...] = face * key_ref[...]
    packed = jnp.dot(compact_ref[...], rows.astype(BF), preferred_element_type=F32)
    held = packed[:BLOCK]
    lifted = packed[BLOCK:]
    lane = iota((BLOCK, LANES), 1)
    line = iota((BLOCK, LANES), 0)

    def key_row(ref, index):
        return jnp.where(line == index, jnp.sum(face * ref[...], axis=0, keepdims=True), 0.0)

    def main(block, far):
        return pltpu.roll(jnp.where(lane < KEY_LANE, block, 0.0), KEY_LANE if far else 0, axis=1)

    def tail(block, index):
        ends = jnp.where((lane >= KEY_LANE) & (lane < face_width), block, 0.0)
        place = LANES - KEY_LANE + 2 * index * WIDE
        upper = pltpu.roll(ends[:GROUP], place % LANES, axis=1)
        return upper + pltpu.roll(ends[GROUP:], (place + WIDE) % LANES, axis=1)

    up_keys = key_row(up_ref, BLOCK - 1)
    own_out[:BLOCK] = (main(held, False) + key_row(own_ref, BLOCK - 1)).astype(BF)
    own_out[BLOCK : 2 * BLOCK] = (main(lifted, False) - pltpu.roll(up_keys, KEY_LANE, axis=1)).astype(BF)
    none = jnp.zeros((GROUP, LANES), F32)
    own_out[2 * BLOCK :] = jnp.concatenate([tail(held, 0) + tail(lifted, 1), none], axis=0).astype(BF)
    up_out[:BLOCK] = (main(lifted, True) + up_keys).astype(BF)
    up_out[BLOCK:] = jnp.concatenate([tail(lifted, 2), none], axis=0).astype(BF)
    down_out[:BLOCK] = (main(held, True) + key_row(down_ref, BLOCK - 1)).astype(BF)
    down_out[BLOCK:] = jnp.concatenate([tail(held, 3), none], axis=0).astype(BF)


def first_terms(face_width, *arrays):
    width = arrays[2].shape[1]

    def kernel(*refs):
        first_kernel(face_width, *refs)

    return pl.pallas_call(
        kernel,
        out_shape=(
            jax.ShapeDtypeStruct((3 * BLOCK, LANES), BF),
            jax.ShapeDtypeStruct((2 * BLOCK, LANES), BF),
            jax.ShapeDtypeStruct((2 * BLOCK, LANES), BF),
            jax.ShapeDtypeStruct((ROWS, LANES), F32),
            jax.ShapeDtypeStruct((ROWS, LANES), F32),
        ),
        scratch_shapes=[pltpu.VMEM((GROUP, width), F32), pltpu.VMEM((ROWS, LANES), F32)],
        compiler_params=params(),
        name="first_terms",
    )(*arrays)


def pack_kernel(own_ref, below_ref, above_ref, out_ref):
    own = own_ref[...].astype(F32)
    below = below_ref[...].astype(F32)
    above = above_ref[...].astype(F32)
    start = own[:BLOCK] + below[:BLOCK]
    middle = own[BLOCK : 2 * BLOCK] + above[:BLOCK]
    ends = own[2 * BLOCK :] + below[BLOCK:] + above[BLOCK:]
    rows = jnp.concatenate([start, middle, ends[:GROUP]], axis=0).astype(BF)
    for d in range(out_ref.shape[0]):
        out_ref[d] = rows


def pack(dom_count, own, below, above):
    return pl.pallas_call(
        pack_kernel,
        out_shape=jax.ShapeDtypeStruct((dom_count, PACKED, LANES), BF),
        compiler_params=params(4),
        name="pack",
    )(own, below, above)


def second_kernel(
    face_width, slab_ref, terms_ref, key_ref, schur_a, schur_b, put_ref, code_ref, held_out, lifted_out, wide, tall
):
    devices = slab_ref.shape[0]
    depth = devices * BLOCK
    chunks = depth // LANES
    start = slab_ref[:, :BLOCK, :].reshape(depth, LANES)
    middle = slab_ref[:, BLOCK : 2 * BLOCK, :].reshape(depth, LANES)
    ends = slab_ref[:, 2 * BLOCK :, :].astype(F32)
    ends = jnp.concatenate([ends, ends], axis=1).reshape(depth, LANES)
    wanted = ((iota((depth, LANES), 1) & WIDE) != 0) == ((iota((depth, LANES), 0) & GROUP) != 0)
    ends = jnp.where(wanted, ends, 0.0).astype(BF)
    shape = (2 * GROUP, depth)
    line = iota(shape, 0)
    column = iota(shape, 1)
    group = 2 * (line & (GROUP - 1)) + (line >> 3)
    chosen = ((column & (BLOCK - 1)) == BLOCK - 1) & ((column >> 6) == group)
    chosen = jnp.where(chosen, 1.0, 0.0).astype(BF)
    lane = iota((GROUP, LANES), 1)
    key = key_ref[...]

    def block_keys(rows):
        found = jnp.dot(chosen, rows, preferred_element_type=F32)
        low, high = found[:GROUP], found[GROUP:]
        near = jnp.where(lane < KEY_LANE, low, pltpu.roll(high, KEY_LANE, axis=1))
        far = jnp.where(lane < KEY_LANE, pltpu.roll(low, KEY_LANE, axis=1), high)
        return near, far

    outer_keys = block_keys(start)
    inner_keys = block_keys(middle)
    keys = (outer_keys[0], inner_keys[0], outer_keys[1], inner_keys[1])

    def match(b):
        return jnp.concatenate(
            [jnp.where(key == keys[b][c : c + 1], 1.0, 0.0).astype(BF) for c in range(chunks)], axis=1
        )

    matches = [match(b) for b in range(4)]
    outer = jnp.dot(jnp.concatenate([matches[0], matches[2]], axis=0), start, preferred_element_type=F32)
    inner = jnp.dot(jnp.concatenate([matches[1], matches[3]], axis=0), middle, preferred_element_type=F32)
    last = jnp.dot(jnp.concatenate(matches, axis=0), ends, preferred_element_type=F32)
    lane = iota((ROWS, LANES), 1)
    near = outer[:ROWS] + inner[:ROWS]
    far = outer[ROWS:] + inner[ROWS:]
    both = jnp.where(lane < KEY_LANE, near + pltpu.roll(far, KEY_LANE, axis=1), 0.0)
    for b in range(4):
        line = last[b * ROWS : (b + 1) * ROWS]
        place = LANES + KEY_LANE - 2 * b * WIDE
        moved = pltpu.roll(line, place % LANES, axis=1) + pltpu.roll(line, (place - WIDE) % LANES, axis=1)
        both = both + jnp.where((lane >= KEY_LANE) & (lane < face_width), moved, 0.0)
    first = terms_ref[...]
    residual = both + (first - first.astype(BF).astype(F32))
    vectors = gather_wide(residual, wide, face_width)
    wide[...] = products(vectors, schur_a, schur_b)
    second = split_rows(wide, tall, face_width)
    pair = jnp.concatenate([first, second], axis=1)
    placed = exact_dot(put_ref[...], pair)
    positions = held_out.shape[0]
    held_out[...] = placed[:positions]
    codes = jnp.concatenate([code_ref[...], code_ref[...]], axis=1)[:1]
    lifted_out[...] = jnp.where(iota(lifted_out.shape, 0) == BLOCK - 1, codes, placed[positions:])


def second_terms(face_width, positions, *arrays):
    width = arrays[3].shape[1]

    def kernel(*refs):
        second_kernel(face_width, *refs)

    return pl.pallas_call(
        kernel,
        out_shape=(
            jax.ShapeDtypeStruct((positions, 2 * LANES), F32),
            jax.ShapeDtypeStruct((BLOCK, 2 * LANES), F32),
        ),
        scratch_shapes=[pltpu.VMEM((GROUP, width), F32), pltpu.VMEM((ROWS, LANES), F32)],
        compiler_params=params(),
        name="second_terms",
    )(*arrays)


def merge_kernel(held_ref, raised_ref, out_ref):
    raised = raised_ref[...]
    code = raised[BLOCK - 1 :, : 3 * BLOCK]
    place = iota((out_ref.shape[0], 3 * BLOCK), 0).astype(F32)
    onehot = jnp.where(place == code, 1.0, 0.0)
    out_ref[...] = held_ref[...] + exact_dot(onehot.astype(BF), raised)


def merge(held, raised):
    return pl.pallas_call(
        merge_kernel,
        out_shape=jax.ShapeDtypeStruct(held.shape, F32),
        compiler_params=params(4),
        name="merge",
    )(held, raised)


def collect_kernel(arrived_ref, slots_ref, residual_ref, image_ref, slots):
    faces, width = residual_ref.shape
    onehot = face_onehot(slots_ref, slots, arrived_ref.shape[0])
    positions = onehot.shape[0]
    onehot = jnp.concatenate([onehot, jnp.zeros((positions, LANES - BLOCK), F32)], axis=1)
    onehot = jnp.concatenate([onehot] * 4, axis=0).T[:BLOCK, : 3 * positions].astype(BF)
    total = exact_dot(onehot, arrived_ref[...])
    residual_ref[...] = total[:faces, :width]
    image_ref[...] = total[:faces, LANES : LANES + width]


def collect(arrived, slots, faces, width):
    out = jax.ShapeDtypeStruct((faces, width), F32)
    return pl.pallas_call(
        collect_kernel,
        out_shape=(out, out),
        scratch_shapes=[pltpu.VMEM((2, BLOCK), jnp.int32)],
        compiler_params=params(4),
        name="collect",
    )(arrived, slots)


def on_device(
    local_inverse,
    local_trace,
    trace_local,
    trace_trace,
    local_rhs,
    trace_rhs,
    trace_state,
    side_owner,
    side_slot,
    face_slots,
):
    dom_count = lax.axis_size("dom")
    faces, face_width = trace_state.shape
    positions = 2 * dom_count
    slots = face_slots.T
    blocks = (local_inverse, jnp.swapaxes(local_trace, 1, 2), trace_local, trace_trace)
    outgoing = spread(slots, trace_state, positions)
    here = exchange(outgoing.reshape(dom_count, 2, LANES)).reshape(positions, LANES)
    elements = local_inverse.shape[0]
    early = elements - max(elements // 5, 1)
    schur_a, condensed_a, pick, put, compact, codes, own_keys, up_keys, down_keys, keys = condense(
        0, early, dom_count, blocks, (local_rhs, trace_rhs, side_owner, side_slot)
    )
    here, schur_a, boundary = lax.optimization_barrier((here, schur_a, trace_rhs))
    above = shift(here, -1)
    schur_b, condensed_b = condense(
        early, elements - early, dom_count, blocks, (local_rhs, boundary), (schur_a,)
    )
    own, lifted, held, terms, key = first_terms(
        face_width,
        here,
        above,
        schur_a,
        schur_b,
        condensed_a,
        condensed_b,
        pick,
        compact,
        own_keys,
        up_keys,
        down_keys,
        keys,
    )
    slab = exchange(pack(dom_count, own, shift(lifted, 1), shift(held, -1)))
    stay, rise = second_terms(face_width, positions, slab, terms, key, schur_a, schur_b, put, codes)
    arriving = merge(stay, shift(rise, 1))
    arrived = exchange(arriving.reshape(dom_count, 2, 2 * LANES)).reshape(positions, 2 * LANES)
    return collect(arrived, slots, faces, face_width)


def solution(mesh):
    both = ("grp", "dom")
    blocks = (P(both, None, None),) * 4
    rows = (P(both, None),) * 6
    return jax.shard_map(
        on_device,
        mesh=mesh,
        in_specs=blocks + rows,
        out_specs=(P(both, None), P(both, None)),
        check_vma=False,
    )
```
